32 devices in a mesh: batch: 8 (over y, x, core), rows: 4 (over z).
Axes of the slice: x: 2, y: 2, z: 4, core: 2. Of those that a mesh axis runs over, the one named last changes fastest.
Arguments:
- images: bfloat16 [160, 16, 14, 1536], P('batch', 'rows'), may hold values from -6 to 6
- orientation: int32 [160], P('batch'), may hold values from 0 to 1
- cotangent: bfloat16 [160, 16, 14, 1536], P('batch', 'rows'), may hold values from -6 to 6
- proj_in: bfloat16 [1536, 768], replicated, may hold values from -0.15625 to 0.15625
- bias_in: float32 [768], replicated, may hold values from -3 to 3
- gain_in: float32 [768], replicated, may hold values from 0.1 to 1.9
- conv_one: bfloat16 [9, 128, 768], replicated, may hold values from -0.1875 to 0.1875
- bias_one: float32 [768], replicated, may hold values from -3 to 3
- gain_one: float32 [768], replicated, may hold values from 0.1 to 1.9
- conv_two: bfloat16 [9, 128, 768], replicated, may hold values from -0.1875 to 0.1875
- bias_two: float32 [768], replicated, may hold values from -3 to 3
- gain_two: float32 [768], replicated, may hold values from 0.1 to 1.9
- proj_out: bfloat16 [768, 1536], replicated, may hold values from -0.21875 to 0.21875
- bias_out: float32 [1536], replicated, may hold values from -3 to 3
- gain_out: float32 [1536], replicated, may hold values from 0.1 to 1.9
- squeeze_weight: bfloat16 [1536, 768], replicated, may hold values from -0.15625 to 0.15625
- squeeze_bias: float32 [768], replicated, may hold values from -3 to 3
- excite_weight: bfloat16 [768, 1536], replicated, may hold values from -0.21875 to 0.21875
- excite_bias: float32 [1536], replicated, may hold values from -3 to 3
- skip_gain: float32 [1], replicated, may hold values from 2 to 5
Outputs:
- output: bfloat16 [160, 16, 14, 1536], P('batch', 'rows')
- grad_images: bfloat16 [160, 16, 14, 1536], P('batch', 'rows')
- grad_proj_in: float32 [1536, 768], replicated
- grad_bias_in: float32 [768], replicated
- grad_gain_in: float32 [768], replicated
- grad_conv_one: float32 [9, 128, 768], replicated
- grad_bias_one: float32 [768], replicated
- grad_gain_one: float32 [768], replicated
- grad_conv_two: float32 [9, 128, 768], replicated
- grad_bias_two: float32 [768], replicated
- grad_gain_two: float32 [768], replicated
- grad_proj_out: float32 [768, 1536], replicated
- grad_bias_out: float32 [1536], replicated
- grad_gain_out: float32 [1536], replicated
- grad_squeeze_weight: float32 [1536, 768], replicated
- grad_squeeze_bias: float32 [768], replicated
- grad_excite_weight: float32 [768, 1536], replicated
- grad_excite_bias: float32 [1536], replicated
- grad_skip_gain: float32 [1], replicated
The draws below stay inside these ranges and needn't reach their ends.
Inputs may be any that keep to these rules, and one draw needn't show every extreme that they name: Each image's orientation.
All inputs are finite; a program needn't handle non-finite values.
Results may differ from the reference program's by a relative error of at most 0.015.
The reference program's roundings to bfloat16 on the way count: a program that leaves them out, or rounds other values in their place, can miss the bound.
Values may be sent and summed in bfloat16 or wider, within the bound.
No kernel may reach another device: no remote copies, remote signals or barrier semaphores. Data moves between devices by JAX's collectives and lax.ppermute only.
A program may use at most 256 MiB of HBM per device.

```python
import jax
import jax.numpy as jnp
import numpy as np
from jax import lax

C = 1536
B = 768
GW = 128
SEH = 768
IMG_DEV = 20
ROW_SLOTS = 4
COL_SLOTS = 14
PIXELS = 140
IMAGES = 160
SLOT_ROWS = 16
N_BATCH = 8
N_ROWS = 4


def plant(values, stream_key, smallest, high):
    place = [jax.random.randint(jax.random.fold_in(stream_key, axis), (), 0, length) for axis, length in enumerate(values.shape)]
    main_axis = values.shape.index(max(values.shape))
    next_to = place[:main_axis] + [(place[main_axis] + 1) % values.shape[main_axis]] + place[main_axis + 1:]
    return values.at[tuple(place)].set(smallest).at[tuple(next_to)].set(high)


def steps_of(key, shape, pieces, smallest, top_value):
    loudness, own = 1.0, jax.random.fold_in(key, 6)
    for axis_at, shards_of in pieces:
        steps = jnp.exp(jax.random.uniform(jax.random.fold_in(own, axis_at), (shards_of,), jnp.float32, smallest / len(pieces), top_value / len(pieces)))
        loudness = loudness * jnp.repeat(steps, shape[axis_at] // shards_of).reshape([-1 if axis == axis_at else 1 for axis in range(len(shape))])
    return loudness


def gaussian(stream_key, extent, scale, bound, pieces=(), kind=jnp.bfloat16):
    factor_of = steps_of(stream_key, extent, pieces, -0.22, 0.18) if pieces else 1.0
    drawn = jax.random.normal(stream_key, extent, jnp.float32) * scale * factor_of
    return jnp.minimum(jnp.maximum(drawn, -bound), bound).astype(kind)


def setup_inputs(seed: int = 0) -> dict:
    seeds = jax.random.split(jax.random.key(seed), 21)
    images = gaussian(seeds[0], (IMAGES, SLOT_ROWS, COL_SLOTS, C), 1.0, 6.0, ((0, 8), (1, 4)))
    orientation = plant(jax.random.randint(seeds[1], (IMAGES,), 0, 2), jax.random.fold_in(seeds[1], 1), 0, 1).astype(jnp.int32)
    cotangent = gaussian(seeds[2], (IMAGES, SLOT_ROWS, COL_SLOTS, C), 1.0, 6.0, ((0, 8), (1, 4)))
    proj_in = gaussian(seeds[3], (C, B), C ** -0.5, 0.15625)
    bias_in = gaussian(seeds[4], (B,), 0.5, 3.0, (), jnp.float32)
    gain_in = jnp.clip(1.0 + 0.18 * jax.random.normal(seeds[5], (B,), jnp.float32), 0.1, 1.9)
    conv_one = gaussian(seeds[6], (9, GW, B), (9 * GW) ** -0.5, 0.1875)
    bias_one = gaussian(seeds[7], (B,), 0.5, 3.0, (), jnp.float32)
    gain_one = jnp.clip(1.0 + 0.18 * jax.random.normal(seeds[8], (B,), jnp.float32), 0.1, 1.9)
    conv_two = gaussian(seeds[9], (9, GW, B), (9 * GW) ** -0.5, 0.1875)
    bias_two = gaussian(seeds[10], (B,), 0.5, 3.0, (), jnp.float32)
    gain_two = jnp.clip(1.0 + 0.18 * jax.random.normal(seeds[11], (B,), jnp.float32), 0.1, 1.9)
    proj_out = gaussian(seeds[12], (B, C), B ** -0.5, 0.21875)
    bias_out = gaussian(seeds[13], (C,), 0.5, 3.0, (), jnp.float32)
    gain_out = jnp.clip(1.0 + 0.18 * jax.random.normal(seeds[14], (C,), jnp.float32), 0.1, 1.9)
    squeeze_weight = gaussian(seeds[15], (C, SEH), C ** -0.5, 0.15625)
    squeeze_bias = gaussian(seeds[16], (SEH,), 0.5, 3.0, (), jnp.float32)
    excite_weight = gaussian(seeds[17], (SEH, C), SEH ** -0.5, 0.21875)
    excite_bias = gaussian(seeds[18], (C,), 0.5, 3.0, (), jnp.float32)
    skip_gain = jnp.clip(jax.random.uniform(seeds[19], (1,), jnp.float32, 2.0, 5.0), 2.0, 5.0)
    return dict(images=images, orientation=orientation, cotangent=cotangent, proj_in=proj_in, bias_in=bias_in, gain_in=gain_in, conv_one=conv_one, bias_one=bias_one, gain_one=gain_one, conv_two=conv_two, bias_two=bias_two, gain_two=gain_two, proj_out=proj_out, bias_out=bias_out, gain_out=gain_out, squeeze_weight=squeeze_weight, squeeze_bias=squeeze_bias, excite_weight=excite_weight, excite_bias=excite_bias, skip_gain=skip_gain)


GAMMA = 1.7015043497
BETA_SCALE = 0.9128709291752769
ALPHA = 0.2
WS_EPS = 1e-05
PRECISE = lax.Precision.HIGHEST

@jax.custom_vjp
def low(v):
    return lax.optimization_barrier(v.astype(jnp.bfloat16)).astype(jnp.float32)

@jax.custom_vjp
def low_back(v):
    return v

def low_keep(v):
    return (low(v), None)

def low_pass(kept, grad):
    return (grad,)

def back_keep(v):
    return (v, None)

def back_low(kept, grad):
    return (low(grad),)
low.defvjp(low_keep, low_pass)
low_back.defvjp(back_keep, back_low)

def gelu_scaled(signal):
    return GAMMA * jax.nn.gelu(signal, approximate=False)

def standardize(weight, gain_vec, fan_axes):
    center = weight - lax.optimization_barrier(jnp.mean(weight, axis=fan_axes, keepdims=True))
    spread = lax.optimization_barrier(jnp.mean(center * center, axis=fan_axes, keepdims=True))
    fan_in = 1
    for member in fan_axes:
        fan_in = fan_in * weight.shape[member]
    return gain_vec * center * lax.rsqrt(spread * fan_in + WS_EPS)

def row_tables(height, slot_rows, col_slots, row_slots):
    base_rows = height // 4
    extra_rows = height % 4
    forward_map = np.zeros((col_slots,), np.int32)
    back_map = np.zeros((slot_rows,), np.int32)
    slot_valid = np.zeros((slot_rows,), np.float32)
    offset = 0
    for device in range(4):
        counted = base_rows + (1 if device < extra_rows else 0)
        for within in range(counted):
            forward_map[offset + within] = row_slots * device + within
            back_map[row_slots * device + within] = offset + within
            slot_valid[row_slots * device + within] = 1.0
        offset = offset + counted
    return (forward_map, back_map, slot_valid)

def grouped(act, weight_hat):
    height = act.shape[1]
    width = act.shape[2]
    padded = jnp.pad(act, ((0, 0), (1, 1), (1, 1), (0, 0)))
    stacked = jnp.stack([padded[:, 1 + row_step:1 + row_step + height, 1 + col_step:1 + col_step + width] for row_step in (-1, 0, 1) for col_step in (-1, 0, 1)], axis=3)
    groups = weight_hat.shape[2] // GW
    stacked = stacked.reshape(stacked.shape[:4] + (groups, GW))
    kernel = weight_hat.reshape(9, GW, groups, GW)
    result = jnp.einsum('nhwkgi,kigo->nhwgo', stacked, kernel, precision=PRECISE)
    return result.reshape(act.shape[:3] + (groups * GW,))

def forward(params, slots, orient, tables):
    proj_in, bias_in, gain_in, conv_one, bias_one, gain_one, conv_two, bias_two, gain_two, proj_out, bias_out, gain_out, squeeze_weight, squeeze_bias, excite_weight, excite_bias, skip_gain = params
    short_fwd, short_back, short_valid, long_fwd, long_back, long_valid = tables
    is_short = orient == 0
    height = jnp.where(is_short, 10, 14)
    width = 24 - height
    fwd_map = jnp.where(is_short[:, None], short_fwd[None], long_fwd[None]).astype(jnp.int32)
    back_map = jnp.where(is_short[:, None], short_back[None], long_back[None]).astype(jnp.int32)
    valid = jnp.where(is_short[:, None], short_valid[None], long_valid[None])
    compact = jnp.take_along_axis(slots, fwd_map[:, :, None, None], axis=1)
    line_ids = jnp.arange(COL_SLOTS)
    mask_c = ((line_ids[None, :, None] < height[:, None, None]) & (line_ids[None, None, :] < width[:, None, None])).astype(jnp.float32)[..., None]
    act_zero = low(gelu_scaled(compact) * BETA_SCALE * mask_c)
    hat_in = low(standardize(proj_in, gain_in, (0,)))
    hat_one = low(standardize(conv_one, gain_one, (0, 1)))
    hat_two = low(standardize(conv_two, gain_two, (0, 1)))
    hat_out = low(standardize(proj_out, gain_out, (0,)))
    pre_one = low_back(jnp.einsum('nhwc,cb->nhwb', act_zero, hat_in, precision=PRECISE) + bias_in)
    act_one = low(gelu_scaled(pre_one) * mask_c)
    pre_two = low_back(grouped(act_one, hat_one) + bias_one)
    act_two = low(gelu_scaled(pre_two) * mask_c)
    pre_three = low_back(grouped(act_two, hat_two) + bias_two)
    act_three = low(gelu_scaled(pre_three) * mask_c)
    pre_four = low_back(jnp.einsum('nhwb,bc->nhwc', act_three, hat_out, precision=PRECISE) + bias_out)
    pooled = lax.optimization_barrier(jnp.sum(pre_four * mask_c, axis=(1, 2))) / PIXELS
    squeezed = jnp.dot(pooled, squeeze_weight, precision=PRECISE) + squeeze_bias
    hidden_se = jax.nn.gelu(squeezed, approximate=False)
    excited = jnp.dot(hidden_se, excite_weight, precision=PRECISE) + excite_bias
    gate = 2.0 * jax.nn.sigmoid(excited)
    mixed = compact + ALPHA * skip_gain[0] * pre_four * gate[:, None, None, :]
    slot_mask = valid[:, :, None] * (line_ids[None, None, :] < width[:, None, None]).astype(jnp.float32)
    back_slots = jnp.take_along_axis(mixed, back_map[:, :, None, None], axis=1)
    return back_slots * slot_mask[..., None]

def reference(images, orientation, cotangent, proj_in, bias_in, gain_in, conv_one, bias_one, gain_one, conv_two, bias_two, gain_two, proj_out, bias_out, gain_out, squeeze_weight, squeeze_bias, excite_weight, excite_bias, skip_gain):
    slot_rows = ROW_SLOTS * N_ROWS
    short_tab = row_tables(10, slot_rows, COL_SLOTS, ROW_SLOTS)
    long_tab = row_tables(14, slot_rows, COL_SLOTS, ROW_SLOTS)
    tables = tuple((jnp.asarray(table) for table in short_tab + long_tab))
    params = tuple((member.astype(jnp.float32) for member in (proj_in, bias_in, gain_in, conv_one, bias_one, gain_one, conv_two, bias_two, gain_two, proj_out, bias_out, gain_out, squeeze_weight, squeeze_bias, excite_weight, excite_bias, skip_gain)))
    group_shape = (N_BATCH, IMG_DEV, slot_rows, COL_SLOTS, C)
    slots_all = images.astype(jnp.float32).reshape(group_shape)
    cot_all = cotangent.astype(jnp.float32).reshape(group_shape)
    orient_all = orientation.reshape(N_BATCH, IMG_DEV)

    def step(totals, inputs):
        slots, orient, cot = inputs

        def local_forward(weights, values):
            return forward(weights, values, orient, tables)
        mixed, pull = jax.vjp(local_forward, params, slots)
        grad_params, grad_slots = pull(cot)
        totals = jax.tree.map(lambda left, right: left + right, totals, grad_params)
        return (totals, (mixed, grad_slots))
    zeros = jax.tree.map(jnp.zeros_like, params)
    totals, (mixed_all, grad_all) = lax.scan(step, zeros, (slots_all, orient_all, cot_all))
    full_shape = images.shape
    output = mixed_all.reshape(full_shape).astype(jnp.bfloat16)
    grad_images = grad_all.reshape(full_shape).astype(jnp.bfloat16)
    return (output, grad_images) + tuple(totals)
```

```python
from functools import partial

import jax
import jax.numpy as jnp
from jax import lax
from jax.experimental import pallas as pl
from jax.experimental.pallas import tpu as pltpu
from jax.sharding import PartitionSpec as P

GW = 128
ROW_SLOTS = 4
COL_SLOTS = 14
PITCH = 16
ROWS_IMG = ROW_SLOTS * PITCH
TILE_IMG = ROWS_IMG + 2 * PITCH
PIXELS = 140
STEP = 5
CHUNKS = 2

GAMMA = 1.7015043497
BETA_SCALE = 0.9128709291752769
ALPHA = 0.2
WS_EPS = 1e-05
ROOT_HALF = 0.7071067811865476
INV_ROOT_TWO_PI = 0.3989422804014327
BF = jnp.bfloat16
F32 = jnp.float32
NN = (((1,), (0,)), ((), ()))
NT = (((1,), (1,)), ((), ()))
TN = (((0,), (0,)), ((), ()))
HBM = pltpu.HBM
SMALL = pl.CostEstimate(flops=1, bytes_accessed=1, transcendentals=0)
PARAMS = pltpu.CompilerParams(vmem_limit_bytes=28 * 2**20)


def dot(left, right, dims=NN):
    return lax.dot_general(left, right, dims, preferred_element_type=F32)


def normal_parts(signal):
    phi = 0.5 + 0.5 * lax.erf(signal * ROOT_HALF)
    bell = jnp.exp(-0.5 * signal * signal) * INV_ROOT_TWO_PI
    return phi, bell


def gelu_and_slope(signal):
    phi, bell = normal_parts(signal)
    return (GAMMA * signal) * phi, GAMMA * (phi + signal * bell)


def at_row(index):
    return pl.ds(pl.multiple_of(index * PITCH, PITCH), PITCH)


def lanes(mask, width):
    return jnp.concatenate([mask] * (width // 128), axis=1)


def slot_width(counts, widths, image, slot):
    return jnp.where(slot < counts[image], widths[image], 0)


def below(limit, shape):
    return lax.broadcasted_iota(jnp.int32, shape, 0) < limit


def fill_mask(counts, widths, base, mask_ref):
    for image in range(STEP):
        for slot in range(ROW_SLOTS):
            limit = slot_width(counts, widths, base + image, slot)
            row = image * ROW_SLOTS + slot
            mask_ref[row * PITCH : (row + 1) * PITCH, :] = below(limit, (PITCH, 128)).astype(F32)


def lane_tiles(width):
    return [(tile, slice(tile * 128, (tile + 1) * 128)) for tile in range(width // 128)]


def unpack_image(slots_ref, image, flat_ref):
    for col in range(COL_SLOTS):
        value = slots_ref[image, col].astype(F32)
        for tile, span in lane_tiles(value.shape[1]):
            flat_ref[tile, col * ROW_SLOTS : (col + 1) * ROW_SLOTS, :] = value[:, span]


def pack_image(flat_ref, slots_ref, image):
    for col in range(COL_SLOTS):
        rows = slice(col * ROW_SLOTS, (col + 1) * ROW_SLOTS)
        value = [flat_ref[tile, rows, :] for tile in range(flat_ref.shape[0])]
        slots_ref[image, col] = jnp.concatenate(value, axis=1).astype(BF)


def read_slot(flat_ref, slot):
    rows = pl.ds(slot, PITCH, stride=ROW_SLOTS)
    return jnp.concatenate([flat_ref[tile, rows, :] for tile in range(flat_ref.shape[0])], axis=1)


def write_slot(flat_ref, slot, value):
    rows = pl.ds(slot, PITCH, stride=ROW_SLOTS)
    for tile, span in lane_tiles(value.shape[1]):
        flat_ref[tile, rows, :] = value[:, span]


def clear_tail(flat_ref):
    first = ROW_SLOTS * COL_SLOTS
    flat_ref[:, first:, :] = jnp.zeros((flat_ref.shape[0], ROWS_IMG - first, 128), F32)


def store_edges(scalars, base, act_ref, even_ref, odd_ref):
    counts, _, place = scalars
    odd = place[0] == 1
    for image in range(STEP):
        dest = slice(image * PITCH, (image + 1) * PITCH)
        first = act_ref[image * ROWS_IMG : image * ROWS_IMG + PITCH, :]
        last = act_ref[at_row(image * ROW_SLOTS + counts[base + image] - 1), :]
        even_ref[dest, :] = jnp.where(odd, first, last)
        odd_ref[dest, :] = jnp.where(odd, last, first)


def fill_tile(scalars, base, act_ref, even_ref, odd_ref, tile_ref):
    counts, _, place = scalars
    odd = place[0] == 1
    tile_rows = TILE_IMG // PITCH
    for image in range(act_ref.shape[0] // ROWS_IMG):
        start = image * TILE_IMG
        rim = slice(image * PITCH, (image + 1) * PITCH)
        even, other = even_ref[rim, :], odd_ref[rim, :]
        tile_ref[start : start + PITCH, :] = jnp.where(odd, even, other)
        tile_ref[start + PITCH : start + PITCH + ROWS_IMG, :] = act_ref[
            image * ROWS_IMG : (image + 1) * ROWS_IMG, :
        ]
        tile_ref[start + PITCH + ROWS_IMG : start + TILE_IMG, :] = jnp.zeros(
            (PITCH, act_ref.shape[1]), act_ref.dtype
        )
        tile_ref[at_row(image * tile_rows + counts[base + image] + 1), :] = jnp.where(odd, other, even)


def group_cat(tile_ref, images, group):
    cols = slice(group * GW, (group + 1) * GW)
    return jnp.concatenate(
        [
            jnp.concatenate(
                [
                    tile_ref[
                        image * TILE_IMG + shift * PITCH : image * TILE_IMG + shift * PITCH + ROWS_IMG,
                        cols,
                    ]
                    for image in range(images)
                ],
                axis=0,
            )
            for shift in range(3)
        ],
        axis=1,
    )


def conv_group(tile_ref, images, group, weight, dims):
    wide = dot(group_cat(tile_ref, images, group), weight, dims)
    rows = wide.shape[0]
    return (
        wide[:, GW : 2 * GW]
        + pltpu.roll(wide[:, :GW], 1, 0)
        + pltpu.roll(wide[:, 2 * GW :], rows - 1, 0)
    )


def prep_flat_kernel(weight_ref, gain_ref, hat_ref, stat_ref):
    weight = weight_ref[...].astype(F32)
    fan = weight.shape[0]
    mean = jnp.sum(weight, axis=0, keepdims=True) * (1.0 / fan)
    center = weight - mean
    spread = jnp.sum(center * center, axis=0, keepdims=True) * (1.0 / fan)
    inv = lax.rsqrt(spread * fan + WS_EPS)
    gain = gain_ref[...][None, :]
    hat_ref[...] = (gain * center * inv).astype(BF)
    stat_ref[0:1, :] = mean
    stat_ref[1:2, :] = inv
    stat_ref[2:3, :] = gain


def prep_flat(weight, gain):
    fan, width = weight.shape
    block = 256
    return pl.pallas_call(
        prep_flat_kernel,
        grid=(width // block,),
        in_specs=[
            pl.BlockSpec((fan, block), lambda j: (0, j)),
            pl.BlockSpec((block,), lambda j: (j,)),
        ],
        out_specs=[
            pl.BlockSpec((fan, block), lambda j: (0, j)),
            pl.BlockSpec((8, block), lambda j: (0, j)),
        ],
        out_shape=[
            jax.ShapeDtypeStruct((fan, width), BF),
            jax.ShapeDtypeStruct((8, width), F32),
        ],
        compiler_params=PARAMS,
        name="prep_flat",
    )(weight, gain)


def prep_conv_kernel(weight_ref, gain_ref, fwd_ref, stat_ref):
    weight = weight_ref[...].astype(F32)
    fan = 9 * GW
    mean = jnp.sum(jnp.sum(weight, axis=0), axis=0, keepdims=True) * (1.0 / fan)
    center = weight - mean
    spread = jnp.sum(jnp.sum(center * center, axis=0), axis=0, keepdims=True) * (1.0 / fan)
    inv = lax.rsqrt(spread * fan + WS_EPS)
    gain = gain_ref[...][None, :]
    hat = (gain * center * inv).astype(BF)
    for row in range(3):
        for col in range(3):
            rows, cols = slice(row * GW, (row + 1) * GW), slice(col * GW, (col + 1) * GW)
            fwd_ref[0, rows, cols] = hat[3 * row + col]
    stat_ref[0:1, :] = mean
    stat_ref[1:2, :] = inv
    stat_ref[2:3, :] = gain


def prep_conv(weight, gain):
    width = weight.shape[2]
    groups = width // GW
    square = pl.BlockSpec((1, 3 * GW, 3 * GW), lambda j: (j, 0, 0))
    return pl.pallas_call(
        prep_conv_kernel,
        grid=(groups,),
        in_specs=[
            pl.BlockSpec((9, GW, GW), lambda j: (0, 0, j)),
            pl.BlockSpec((GW,), lambda j: (j,)),
        ],
        out_specs=[square, pl.BlockSpec((8, GW), lambda j: (0, j))],
        out_shape=[
            jax.ShapeDtypeStruct((groups, 3 * GW, 3 * GW), BF),
            jax.ShapeDtypeStruct((8, width), F32),
        ],
        compiler_params=PARAMS,
        name="prep_conv",
    )(weight, gain)


def spec_rows(width, offset=0, per=ROWS_IMG):
    return pl.BlockSpec((STEP * per, width), lambda j, *_: (j + offset, 0))


def spec_slots(width, offset):
    return pl.BlockSpec((STEP, COL_SLOTS, ROW_SLOTS, width), lambda j, *_: (j + offset, 0, 0, 0))


def spec_whole(array):
    zeros = (0,) * array.ndim
    return pl.BlockSpec(array.shape, lambda j, *_: zeros)


def spec_sums(width, offset):
    return pl.BlockSpec((8, width), lambda j, *_: (j + offset, 0))


def in_hbm(array):
    return pltpu.with_memory_space_constraint(array, HBM)


def image_call(kernel, name, scalars, steps, inputs, outputs, scratch=(), flops=0, alias=()):
    return pl.pallas_call(
        kernel,
        grid_spec=pltpu.PrefetchScalarGridSpec(
            num_scalar_prefetch=len(scalars),
            grid=(steps,),
            in_specs=[spec for _, spec in inputs],
            out_specs=[spec for _, spec in outputs],
            scratch_shapes=list(scratch),
        ),
        out_shape=[shape for shape, _ in outputs],
        input_output_aliases={len(scalars) + source: target for source, target in alias},
        compiler_params=PARAMS,
        cost_estimate=SMALL,
        name=name,
    )(*scalars, *[array for array, _ in inputs])


def rows_out(steps, width, per=ROWS_IMG, dtype=BF, space=jax.ShapeDtypeStruct):
    return (space((steps * STEP * per, width), dtype), spec_rows(width, 0, per))


def enter_kernel(
    counts, widths, place, image_ref, hat_ref, bias_ref,
    act0_ref, slope0_ref, act1_ref, slope1_ref, even_ref, odd_ref, mask_ref, flat_ref, *, offset,
):
    base = (pl.program_id(0) + offset) * STEP
    fill_mask(counts, widths, base, mask_ref)
    clear_tail(flat_ref)

    def one_image(image, carry):
        unpack_image(image_ref, image, flat_ref)
        for slot in range(ROW_SLOTS):
            value = read_slot(flat_ref, slot)
            keep = below(slot_width(counts, widths, base + image, slot), value.shape)
            value = jnp.where(keep, value, 0.0)
            act, slope = gelu_and_slope(value)
            row = at_row(image * ROW_SLOTS + slot)
            act0_ref[row, :] = (act * BETA_SCALE).astype(BF)
            slope0_ref[row, :] = (slope * BETA_SCALE).astype(BF)
        return carry

    lax.fori_loop(0, STEP, one_image, 0)
    width = act1_ref.shape[1]
    block = 256
    keep = lanes(mask_ref[...], block)
    for start in range(0, width, block):
        cols = slice(start, start + block)
        pre = dot(act0_ref[...], hat_ref[:, cols]) + bias_ref[cols][None, :]
        act, slope = gelu_and_slope(pre)
        act1_ref[:, cols] = (act * keep).astype(BF)
        slope1_ref[:, cols] = (slope * keep).astype(BF)
    store_edges((counts, widths, place), base, act1_ref, even_ref, odd_ref)


def conv_body(tile_ref, weight_ref, bias_ref, out_ref, slope_ref, keep):
    for group in range(weight_ref.shape[0]):
        cols = slice(group * GW, (group + 1) * GW)
        pre = conv_group(tile_ref, STEP, group, weight_ref[group], NN) + bias_ref[cols][None, :]
        act, slope = gelu_and_slope(pre)
        out_ref[:, cols] = (act * keep).astype(BF)
        slope_ref[:, cols] = (slope * keep).astype(BF)


def conv_kernel(
    counts, widths, place, act_ref, up_ref, down_ref, weight_ref, bias_ref,
    out_ref, slope_ref, even_ref, odd_ref, tile_ref, mask_ref, *, offset,
):
    base = (pl.program_id(0) + offset) * STEP
    scalars = (counts, widths, place)
    fill_mask(counts, widths, base, mask_ref)
    fill_tile(scalars, base, act_ref, up_ref, down_ref, tile_ref)
    conv_body(tile_ref, weight_ref, bias_ref, out_ref, slope_ref, mask_ref[...])
    store_edges(scalars, base, out_ref, even_ref, odd_ref)


def leave_kernel(
    counts, widths, place, act_ref, up_ref, down_ref, weight_ref, bias_ref, hat_ref, bias_out_ref, cot_ref,
    out_ref, slope_ref, four_ref, cotp_ref, sum_ref, tile_ref, mask_ref, flat_ref, *, offset,
):
    base = (pl.program_id(0) + offset) * STEP
    fill_mask(counts, widths, base, mask_ref)
    fill_tile((counts, widths, place), base, act_ref, up_ref, down_ref, tile_ref)
    clear_tail(flat_ref)

    def one_image(image, carry):
        unpack_image(cot_ref, image, flat_ref)
        for slot in range(ROW_SLOTS):
            value = read_slot(flat_ref, slot)
            keep = below(slot_width(counts, widths, base + image, slot), value.shape)
            cotp_ref[at_row(image * ROW_SLOTS + slot), :] = jnp.where(keep, value, 0.0).astype(BF)
        return carry

    lax.fori_loop(0, STEP, one_image, 0)
    keep = mask_ref[...]
    conv_body(tile_ref, weight_ref, bias_ref, out_ref, slope_ref, keep)
    width = four_ref.shape[1]
    block = 256
    keep = lanes(keep, block)
    sum_ref[...] = jnp.zeros_like(sum_ref)
    third = sum_ref.shape[1]

    def put(values, image, column):
        row = column // third * STEP + image
        sum_ref[row : row + 1, column % third : column % third + block] = jnp.sum(
            values[image * ROWS_IMG : (image + 1) * ROWS_IMG], axis=0, keepdims=True
        )

    for start in range(0, width, block):
        cols = slice(start, start + block)
        pre = dot(out_ref[...], hat_ref[:, cols]) + bias_out_ref[cols][None, :]
        four_ref[:, cols] = pre.astype(BF)
        held = pre * keep
        cross = pre * cotp_ref[:, cols].astype(F32)
        for image in range(STEP):
            put(held, image, start)
            put(cross, image, width + start)


def unpacked_sums(*sum_refs):
    rows = []
    for sum_ref in sum_refs:
        for step in range(0, sum_ref.shape[0], 16):
            thirds = [sum_ref[step + STEP * t : step + STEP * (t + 1), :] for t in range(3)]
            rows.append(jnp.concatenate(thirds, axis=1))
            rows.append(jnp.zeros((8 - STEP, 3 * sum_ref.shape[1]), F32))
    return jnp.concatenate(rows, axis=0)


def two_pass(left, right, dims=NN):
    high = left.astype(BF)
    low = (left - high.astype(F32)).astype(BF)
    both = dot(jnp.concatenate([high, low], axis=0), right, dims)
    return both[: left.shape[0]] + both[left.shape[0] :]


def gate_kernel(
    sum0_ref, sum1_ref, squeeze_ref, squeeze_bias_ref, excite_ref, excite_bias_ref, skip_ref,
    scale_ref, shift_ref, factor_ref,
):
    width = scale_ref.shape[1]
    skip = skip_ref[0]
    sums = unpacked_sums(sum0_ref, sum1_ref)
    pooled = sums[:, :width] * (1.0 / PIXELS)
    cross = sums[:, width:] * ALPHA
    squeezed = two_pass(pooled, squeeze_ref[...]) + squeeze_bias_ref[...][None, :]
    phi, bell = normal_parts(squeezed)
    hidden = squeezed * phi
    excited = two_pass(hidden, excite_ref[...]) + excite_bias_ref[...][None, :]
    gate = 2.0 * jax.nn.sigmoid(excited)
    dexcite = (cross * skip) * gate * (1.0 - 0.5 * gate)
    dsqueeze = two_pass(dexcite, excite_ref[...], NT) * (phi + squeezed * bell)
    scale_ref[...] = (ALPHA * skip) * gate
    shift_ref[...] = two_pass(dsqueeze, squeeze_ref[...], NT) * (1.0 / PIXELS)
    dskip = jnp.sum(gate * cross, axis=1, keepdims=True)
    high = dskip.astype(BF).astype(F32)
    mid = (dskip - high).astype(BF).astype(F32)
    lane = lax.broadcasted_iota(jnp.int32, (dskip.shape[0], 128), 1)
    pieces = jnp.where(lane == 0, high, jnp.where(lane == 1, mid, dskip - high - mid))
    pieces = jnp.where(lane < 3, pieces, 0.0)
    factor_ref[...] = jnp.concatenate([pooled, dsqueeze, hidden, dexcite, pieces], axis=1).astype(BF)


def turn_kernel(
    counts, widths, place, cotp_ref, scale_ref, shift_ref, hat_ref, slope_ref, *rest, offset
):
    four_ref, three_ref, even_ref, odd_ref, mask_ref = rest[-5:]
    base = (pl.program_id(0) + offset) * STEP
    fill_mask(counts, widths, base, mask_ref)
    for image in range(STEP):
        rows = slice(image * ROWS_IMG, (image + 1) * ROWS_IMG)
        keep = lanes(mask_ref[rows, :], four_ref.shape[1])
        value = cotp_ref[rows, :].astype(F32) * scale_ref[image : image + 1, :]
        value = value + keep * shift_ref[image : image + 1, :]
        four_ref[rows, :] = value.astype(BF)
    width = three_ref.shape[1]
    block = 256
    for start in range(0, width, block):
        cols = slice(start, start + block)
        back = dot(four_ref[...], hat_ref[cols, :], NT)
        three_ref[:, cols] = (back * slope_ref[:, cols].astype(F32)).astype(BF)
    store_edges((counts, widths, place), base, three_ref, even_ref, odd_ref)


def turned(weight_ref, group):
    square = lambda row, col: weight_ref[
        group, (2 - row) * GW : (3 - row) * GW, (2 - col) * GW : (3 - col) * GW
    ]
    return jnp.concatenate(
        [jnp.concatenate([square(row, col) for row in range(3)], axis=1) for col in range(3)], axis=0
    )


def conv_back_kernel(
    counts, widths, place, grad_ref, up_ref, down_ref, weight_ref, slope_ref, *rest, offset, edged
):
    out_ref, *edges, tile_ref = rest[-4:] if edged else rest
    base = (pl.program_id(0) + offset) * STEP
    scalars = (counts, widths, place)
    fill_tile(scalars, base, grad_ref, up_ref, down_ref, tile_ref)
    for group in range(weight_ref.shape[0]):
        cols = slice(group * GW, (group + 1) * GW)
        back = conv_group(tile_ref, STEP, group, turned(weight_ref, group), NT)
        out_ref[:, cols] = (back * slope_ref[:, cols].astype(F32)).astype(BF)
    if edges:
        store_edges(scalars, base, out_ref, *edges)


def grad_image_kernel(counts, widths, place, grad_ref, hat_ref, slope_ref, cotp_ref, *rest, offset):
    out_ref, work_ref, flat_ref = rest[-3:]
    base = (pl.program_id(0) + offset) * STEP
    width = hat_ref.shape[0]
    block = 256
    for start in range(0, width, block):
        cols = slice(start, start + block)
        back = dot(grad_ref[...], hat_ref[cols, :], NT)
        work_ref[:, cols] = back * slope_ref[:, cols].astype(F32) + cotp_ref[:, cols].astype(F32)

    def one_image(image, carry):
        for slot in range(ROW_SLOTS):
            value = work_ref[at_row(image * ROW_SLOTS + slot), :]
            keep = below(slot_width(counts, widths, base + image, slot), value.shape)
            write_slot(flat_ref, slot, jnp.where(keep, value, 0.0))
        pack_image(flat_ref, out_ref, image)
        return carry

    lax.fori_loop(0, STEP, one_image, 0)


def output_kernel(counts, widths, place, image_ref, four_ref, scale_ref, *rest, offset):
    out_ref, flat_ref = rest[-2:]
    base = (pl.program_id(0) + offset) * STEP
    clear_tail(flat_ref)

    def one_image(image, carry):
        unpack_image(image_ref, image, flat_ref)
        for slot in range(ROW_SLOTS):
            value = read_slot(flat_ref, slot)
            four = four_ref[at_row(image * ROW_SLOTS + slot), :].astype(F32)
            keep = below(slot_width(counts, widths, base + image, slot), value.shape)
            value = jnp.where(keep, value + four * scale_ref[pl.ds(image, 1), :], 0.0)
            write_slot(flat_ref, slot, value)
        pack_image(flat_ref, out_ref, image)
        return carry

    lax.fori_loop(0, STEP, one_image, 0)


def split_halves(scratch_ref, core, keep_ref, send_ref):
    keep_ref[...] = scratch_ref[core]
    send_ref[...] = scratch_ref[1 - core]


def weight_flat_kernel(
    need, core, left0, left1, right0, right1, weight_ref, stat_ref, keep_ref, send_ref, vec_ref, scratch_ref
):
    pieces, rows, span = keep_ref.shape

    def store(start, grad):
        for first in range(0, grad.shape[0], rows):
            half, piece = divmod((start // span * grad.shape[0] + first) // rows, pieces)
            scratch_ref[half, piece, :, start % span : start % span + grad.shape[1]] = grad[
                first : first + rows
            ]

    weight_flat_body(need, left0, left1, right0, right1, weight_ref, stat_ref, store, vec_ref)
    split_halves(scratch_ref, core[0], keep_ref, send_ref)


def weight_flat_body(need, left0, left1, right0, right1, weight_ref, stat_ref, store, vec_ref):
    fan, width = weight_ref.shape
    block = 256
    vec_ref[...] = jnp.zeros_like(vec_ref)
    for start in range(0, width, block):
        cols = slice(start, start + block)
        if start == 0:
            need(0, 2)
        ghat = dot(left0[...], right0[:, cols], TN)
        if start == 0:
            need(1, 3)
        ghat = ghat + dot(left1[...], right1[:, cols], TN)
        if start == 0:
            need(4, 5)
        mean, inv, gain = stat_ref[0:1, cols], stat_ref[1:2, cols], stat_ref[2:3, cols]
        center = weight_ref[:, cols].astype(F32) - mean
        along = jnp.sum(ghat * center, axis=0, keepdims=True)
        level = jnp.sum(ghat, axis=0, keepdims=True) * (1.0 / fan)
        grad = ((gain * inv) * (ghat - level - center * (inv * inv * along))).astype(BF)
        store(start, grad)
        total = jnp.sum(right0[:, cols].astype(F32), axis=0, keepdims=True)
        total = total + jnp.sum(right1[:, cols].astype(F32), axis=0, keepdims=True)
        vec_ref[0:1, cols] = total
        vec_ref[1:2, cols] = inv * along


def halves_out(rows, span):
    shape = (4, rows // 8, span)
    return [jax.ShapeDtypeStruct(shape, BF)] * 2, pltpu.VMEM((2, *shape), BF)


def loading(kernel, scalars, loads, order):
    def loaded(*refs):
        heads, sources, rest = refs[:scalars], refs[scalars : scalars + loads], refs[scalars + loads :]
        rest, buffers, arrived = rest[: -loads - 1], rest[-loads - 1 : -1], rest[-1]
        copies = [
            pltpu.make_async_copy(source, buffer, arrived.at[k])
            for k, (source, buffer) in enumerate(zip(sources, buffers))
        ]
        for k in order:
            copies[k].start()

        def need(*which):
            for k in which:
                copies[k].wait()

        kernel(need, *heads, *buffers, *rest)

    return loaded


def weight_call(kernel, name, scalars, inputs, rows, span, width, scratch, order):
    halves, both = halves_out(rows, span)
    return pl.pallas_call(
        loading(kernel, len(scalars), len(inputs), order),
        in_specs=[pl.BlockSpec(memory_space=pltpu.SMEM)] * len(scalars)
        + [pl.BlockSpec(memory_space=HBM)] * len(inputs),
        out_shape=[*halves, jax.ShapeDtypeStruct((8, width), F32)],
        scratch_shapes=[
            both,
            *scratch,
            *[pltpu.VMEM(array.shape, array.dtype) for array in inputs],
            pltpu.SemaphoreType.DMA((len(inputs),)),
        ],
        compiler_params=PARAMS,
        cost_estimate=SMALL,
        name=name,
    )(*scalars, *[in_hbm(array) for array in inputs])


def weight_flat(core, lefts, rights, weight, stat, span, name):
    fan, width = weight.shape
    return weight_call(
        weight_flat_kernel, name, [core], [*lefts, *rights, weight, stat],
        fan * width // span, span, width, [], (0, 2, 1, 3, 4, 5),
    )


def weight_conv_kernel(
    need, core, counts, widths, place, act0, act1, even0, even1, odd0, odd1, grad0, grad1, weight_ref, stat_ref,
    keep_ref, send_ref, vec_ref, scratch_ref, tile_ref,
):
    images = act0.shape[0] // ROWS_IMG
    fan = 9 * GW
    scalars = (counts, widths, place)
    pieces, piece_rows, _ = keep_ref.shape
    need(0, 2, 4)
    fill_tile(scalars, 0, act0, even0, odd0, tile_ref.at[0])
    need(1, 3, 5)
    fill_tile(scalars, images, act1, even1, odd1, tile_ref.at[1])
    need(6, 7, 8, 9)
    vec_ref[...] = jnp.zeros_like(vec_ref)
    for group in range(weight_ref.shape[2] // GW):
        cols = slice(group * GW, (group + 1) * GW)
        ghat = jnp.zeros((3 * GW, 3 * GW), F32)
        total = jnp.zeros((1, GW), F32)
        for index, grad_ref in enumerate((grad0, grad1)):
            grad = grad_ref[:, cols].astype(F32)
            rows = grad.shape[0]
            total = total + jnp.sum(grad, axis=0, keepdims=True)
            wide = jnp.concatenate(
                [
                    pltpu.roll(grad, rows - 1, 0).astype(BF),
                    grad_ref[:, cols],
                    pltpu.roll(grad, 1, 0).astype(BF),
                ],
                axis=1,
            )
            ghat = ghat + dot(group_cat(tile_ref.at[index], images, group), wide, TN)
        mean, inv, gain = stat_ref[0:1, cols], stat_ref[1:2, cols], stat_ref[2:3, cols]
        along = jnp.zeros((1, GW), F32)
        level = jnp.zeros((1, GW), F32)
        centers, taps = [], []
        for tap in range(9):
            row, col = tap // 3, tap % 3
            part = ghat[row * GW : (row + 1) * GW, col * GW : (col + 1) * GW]
            center = weight_ref[tap, :, cols].astype(F32) - mean
            along = along + jnp.sum(part * center, axis=0, keepdims=True)
            level = level + jnp.sum(part, axis=0, keepdims=True)
            centers.append(center)
            taps.append(part)
        level = level * (1.0 / fan)
        slope = inv * inv * along
        for tap in range(9):
            grad = ((gain * inv) * (taps[tap] - level - centers[tap] * slope)).astype(BF)
            row = 0
            while row < GW:
                whole, inside = divmod(tap * GW + row, piece_rows)
                half, piece = divmod(whole, pieces)
                size = min(piece_rows - inside, GW - row)
                scratch_ref[half, piece, inside : inside + size, cols] = grad[row : row + size]
                row += size
        vec_ref[0:1, cols] = total
        vec_ref[1:2, cols] = inv * along
    split_halves(scratch_ref, core[0], keep_ref, send_ref)


def weight_conv(core, scalars, acts, rims, grads, weight, stat, name):
    width = weight.shape[2]
    images = acts[0].shape[0] // ROWS_IMG
    inputs = [*acts, *[r[0] for r in rims], *[r[1] for r in rims], *grads, weight, stat]
    return weight_call(
        weight_conv_kernel, name, [core, *scalars], inputs, 9 * GW, width, width,
        [pltpu.VMEM((2, images * TILE_IMG, width), BF)], (0, 2, 4, 1, 3, 5, 6, 7, 8, 9),
    )


def outer_kernel(factor_ref, out_ref, sum_ref, *skip, start):
    left, right = out_ref.shape
    factor = factor_ref[:, start + left : start + left + right]
    out_ref[...] = dot(factor_ref[:, start : start + left], factor, TN)
    sum_ref[...] = jnp.sum(factor.astype(F32), axis=0)
    for ref in skip:
        pieces = factor_ref[:, factor_ref.shape[1] - 128 :].astype(F32)
        ref[...] = jnp.broadcast_to(jnp.sum(pieces), ref.shape)


def outer(factors, start, left, right, name, skip=False):
    return pl.pallas_call(
        partial(outer_kernel, start=start),
        out_shape=[HBM((left, right), F32), jax.ShapeDtypeStruct((right,), F32)]
        + [jax.ShapeDtypeStruct((8, 128), F32)] * skip,
        compiler_params=PARAMS,
        cost_estimate=SMALL,
        name=name,
    )(factors)


def vector_kernel(core, in_ref, one_ref, two_ref, out_ref, keep_ref, send_ref):
    span = keep_ref.shape[2]
    keep_ref[...] = jnp.zeros_like(keep_ref)
    send_ref[...] = jnp.zeros_like(send_ref)
    rows = [ref[r : r + 1, :] for ref in (in_ref, one_ref, two_ref) for r in range(2)]
    rows += [out_ref[r : r + 1, c : c + span] for r in range(2) for c in range(0, out_ref.shape[1], span)]
    rows.append(jnp.zeros((16 - len(rows), span), F32))
    block = jnp.concatenate(rows, axis=0)
    keep_ref[0] = jnp.where(core[0] == 0, block, 0.0).astype(BF)
    send_ref[0] = jnp.where(core[0] == 0, 0.0, block).astype(BF)


def swap(block, axis, bit):
    count = lax.axis_size(axis)
    return lax.ppermute(block, axis, [(i, i ^ (1 << bit)) for i in range(count)])


def bit_of(axis, bit):
    return ((lax.axis_index(axis) >> bit) & 1).astype(jnp.int32)


def neighbours(even, odd):
    count = lax.axis_size("rows")
    inner = [(i, i + 1) for i in range(1, count - 1, 2)]
    outer_pairs = [(i, i + 1) for i in range(0, count, 2)]
    both = lambda pairs: pairs + [(target, source) for source, target in pairs]
    return lax.ppermute(even, "rows", both(outer_pairs)), lax.ppermute(odd, "rows", both(inner))


def rows_sum(total):
    for bit in range(lax.axis_size("rows").bit_length() - 1):
        total = total + swap(total, "rows", bit)
    return total


def orders():
    bits = lax.axis_size("batch").bit_length() - 1
    middle = 1 + (bits - 1) // 2
    along_x = [("batch", bit) for bit in range(1, middle)]
    along_y = [("batch", bit) for bit in range(middle, bits)]
    along_z = [("rows", bit) for bit in range(lax.axis_size("rows").bit_length() - 1)]
    return [along_x + along_y + along_z, along_y + along_z + along_x]


def swap_way(block, ways, step):
    rows = lax.axis_size("rows")
    pairs = []
    for index in range(lax.axis_size("batch") * rows):
        axis, bit = ways[(index // rows) & 1][step]
        pairs.append((index, index ^ ((rows if axis == "batch" else 1) << bit)))
    return lax.ppermute(block, ("batch", "rows"), pairs)


def small_call(kernel, name, scalars, inputs, outputs):
    return pl.pallas_call(
        kernel,
        in_specs=[pl.BlockSpec(memory_space=pltpu.SMEM)] * len(scalars)
        + [pl.BlockSpec(memory_space=pltpu.VMEM)] * len(inputs),
        out_shape=outputs,
        compiler_params=PARAMS,
        cost_estimate=SMALL,
        name=name,
    )(*scalars, *inputs)


def first_kernel(bits, *refs):
    sources, (kept, send) = refs[:-2], refs[-2:]
    mine = bits[0]
    for second in range(2):
        for index, dest in ((2 * mine + second, kept), (2 * (1 - mine) + second, send)):
            row = 0
            for keep, got in zip(sources[0::2], sources[1::2]):
                rows = keep.shape[1]
                value = keep[index].astype(F32) + got[index].astype(F32)
                dest[second, row : row + rows, :] = value.astype(dest.dtype)
                row += rows


def second_kernel(bits, kept, got, keep, send):
    mine = bits[1]
    keep[...] = kept[mine] + got[mine].astype(F32)
    send[...] = (kept[1 - mine] + got[1 - mine].astype(F32)).astype(BF)


def add_kernel(left, right, out):
    out[...] = (left[...].astype(F32) + right[...].astype(F32)).astype(BF)


def pair_kernel(left, right, out):
    out[0] = left[...]
    out[1] = right[...]


def join_kernel(left, right, out):
    out[0:2] = left[...]
    out[2:4] = right[...]


def spread_kernel(bits, own_ref, other_ref, *outs, vectors):
    pieces, _, span = own_ref.shape
    core = bits[2]
    if vectors:
        outs, lines, table = outs[: -1 - vectors], outs[-1 - vectors : -1], outs[-1]
        outs = [*outs, table]
    for piece in range(pieces):
        place = 2 * (bits[0] ^ (piece >> 1)) + (bits[1] ^ (piece & 1))
        other_place = 2 * (bits[3] ^ (piece >> 1)) + (bits[4] ^ (piece & 1))
        row = 0
        for out in outs:
            rows = out.shape[0] * out.shape[1] // (2 * pieces * span)
            if out.shape[1] == span:
                for half, where, ref in ((core, place, own_ref), (1 - core, other_place, other_ref)):
                    at = pl.ds(pl.multiple_of((half * pieces + where) * rows, rows), rows)
                    out[at, :] = ref[piece, row : row + rows].astype(F32)
            else:
                for half in range(2):

                    @pl.when(core == half)
                    def _(half=half, row=row, out=out, rows=rows):
                        for side, where, ref in ((half, place, own_ref), (1 - half, other_place, other_ref)):
                            at = pl.ds(pl.multiple_of(where * rows, rows), rows)
                            out[at, side * span : (side + 1) * span] = ref[piece, row : row + rows].astype(F32)

            row += rows
    if vectors:
        row = 0
        for out in lines:
            for start in range(0, out.shape[0], span):
                out[start : start + span] = table[row]
                row += 1


def interleave(left, right):
    return [item for pair in zip(left, right) for item in pair]


def ordered(before, after):
    flat_before, tree_before = jax.tree.flatten(before)
    flat_after, tree_after = jax.tree.flatten(after)
    out = lax.optimization_barrier((*flat_before, *flat_after))
    split = len(flat_before)
    return tree_before.unflatten(out[:split]), tree_after.unflatten(out[split:])


class Reduction:
    def __init__(self, *blocks):
        self.landed = False
        self.keep = [keep for keep, _ in blocks]
        self.send = [send for _, send in blocks]
        self.rows = [keep.shape[1] for keep in self.keep]
        rows, span = sum(self.rows), self.keep[0].shape[2]
        self.shape = lambda dtype, *lead: jax.ShapeDtypeStruct((*lead, rows, span), dtype)
        ways = orders()
        core = bit_of("batch", 0)
        mine = [[bit_of(*way[step]) for step in range(2)] for way in ways]
        choose = lambda step, which: jnp.where(core == which, mine[0][step], mine[1][step])
        self.bits = jnp.stack([choose(0, 0), choose(1, 0), core, choose(0, 1), choose(1, 1)])
        across = lambda step: lambda blocks: [swap_way(block, ways, step) for block in blocks]
        chip = lambda blocks: [swap(block, "batch", 0) for block in blocks]
        self.plan = [(chip, self.halve_first), (across(0), self.halve_second), (across(1), self.add_last)]
        self.plan += [(across(step), self.add_all) for step in (2, 3)]
        self.across, self.rest = across, range(4, len(ways[0]))
        self.plan += [(across(1), self.pair), (across(0), self.join), (chip, self.done)]

    def fly(self):
        self.move, self.work = self.plan.pop(0)
        self.got = self.move(self.send)

    def land(self, before):
        before, (self.keep, self.got) = ordered(before, (self.keep, self.got))
        self.work()
        return before

    def hold(self, after):
        self.send, after = ordered(self.send, after)
        return after

    def call(self, kernel, name, bits, left, right, outputs):
        return small_call(kernel, name, bits, interleave(left, right), outputs)

    def halve_first(self):
        outs = [self.shape(F32, 2), self.shape(BF, 2)]
        kept, send = self.call(first_kernel, "halve_first", [self.bits], self.keep, self.got, outs)
        self.keep, self.send = [kept], [send]

    def halve_second(self):
        outs = [self.shape(F32), self.shape(BF)]
        kept, send = self.call(second_kernel, "halve_second", [self.bits], self.keep, self.got, outs)
        self.keep, self.send = [kept], [send]

    def add_last(self):
        self.send = self.call(add_kernel, "add_last", [], self.keep, self.got, [self.shape(BF)])
        self.keep = []

    def add_all(self):
        self.send = self.call(add_kernel, "add_all", [], self.send, self.got, [self.shape(BF)])
        if self.plan[0][1] == self.pair:
            for step in self.rest:
                got = self.across(step)(self.send)
                self.send = self.call(add_kernel, "add_all", [], self.send, got, [self.shape(BF)])

    def pair(self):
        self.send = self.call(pair_kernel, "pair", [], self.send, self.got, [self.shape(BF, 2)])

    def join(self):
        self.send = self.call(join_kernel, "join", [], self.send, self.got, [self.shape(BF, 4)])

    def done(self):
        self.landed = True

    def spread(self, *shapes, vectors=()):
        inputs = [self.send[0], self.got[0]]
        return pl.pallas_call(
            partial(spread_kernel, vectors=len(vectors)),
            in_specs=[pl.BlockSpec(memory_space=pltpu.SMEM)] + [pl.BlockSpec(memory_space=pltpu.VMEM)] * 2,
            out_shape=[HBM(shape, F32) for shape in shapes]
            + [jax.ShapeDtypeStruct(shape, F32) for shape in vectors],
            scratch_shapes=[pltpu.VMEM((128, inputs[0].shape[2]), F32)] if vectors else [],
            compiler_params=PARAMS,
            cost_estimate=SMALL,
            name="spread",
        )(self.bits, *inputs)


def shards(
    images, orientation, cotangent, proj_in, bias_in, gain_in, conv_one, bias_one, gain_one,
    conv_two, bias_two, gain_two, proj_out, bias_out, gain_out, squeeze_weight, squeeze_bias,
    excite_weight, excite_bias, skip_gain,
):
    count = images.shape[0]
    wide, narrow = proj_in.shape
    steps = count // STEP // CHUNKS
    images = images.transpose(0, 2, 1, 3)
    cotangent = cotangent.transpose(0, 2, 1, 3)
    height = jnp.where(orientation == 0, 10, 14).astype(jnp.int32)
    widths = 24 - height
    row_index = lax.axis_index("rows")
    counts = height // 4 + (row_index < height % 4).astype(jnp.int32)
    core = bit_of("batch", 0).reshape(1)
    scalars = (counts, widths, (row_index % 2).astype(jnp.int32).reshape(1))
    mask_scratch = pltpu.VMEM((STEP * ROWS_IMG, 128), F32)
    tile_scratch = pltpu.VMEM((STEP * TILE_IMG, narrow), BF)
    flat_scratch = pltpu.VMEM((wide // 128, ROWS_IMG, 128), F32)
    work = 2 * steps * STEP * ROWS_IMG * wide * narrow
    conv_work = 2 * steps * STEP * ROWS_IMG * 12 * GW * narrow

    hat_in, stat_in = prep_flat(proj_in, gain_in)
    fwd_one, stat_one = prep_conv(conv_one, gain_one)
    fwd_two, stat_two = prep_conv(conv_two, gain_two)
    hat_out, stat_out = prep_flat(proj_out, gain_out)

    chunks = range(CHUNKS)
    rim = lambda: rows_out(steps, narrow, PITCH)
    rim_in = lambda r: [(r[0], spec_rows(narrow, 0, PITCH)), (r[1], spec_rows(narrow, 0, PITCH))]
    big = lambda: rows_out(steps, wide, space=HBM)
    mid = lambda: rows_out(steps, narrow)
    far = lambda: rows_out(steps, narrow, space=HBM)
    act0, slope0, act1, slope1, rims1 = [], [], [], [], []
    for c in chunks:
        a0, s0, a1, s1, *edges = image_call(
            partial(enter_kernel, offset=c * steps), "enter", scalars, steps,
            [(images, spec_slots(wide, c * steps)), (hat_in, spec_whole(hat_in)),
             (bias_in, spec_whole(bias_in))],
            [big(), big(), mid(), far(), rim(), rim()],
            [mask_scratch, flat_scratch], work,
        )
        act0.append(a0), slope0.append(s0), act1.append(a1), slope1.append(s1)
        rims1.append(neighbours(*edges))
    act2, slope2, rims2 = [], [], []
    for c in chunks:
        a2, s2, *edges = image_call(
            partial(conv_kernel, offset=c * steps), "conv_one", scalars, steps,
            [(act1[c], spec_rows(narrow)), *rim_in(rims1[c]), (fwd_one, spec_whole(fwd_one)),
             (bias_one, spec_whole(bias_one))],
            [mid(), far(), rim(), rim()],
            [tile_scratch, mask_scratch], conv_work,
        )
        act2.append(a2), slope2.append(s2)
        rims2.append(neighbours(*edges))
    act3, slope3, four, cotp, sums = [], [], [], [], []
    for c in chunks:
        a3, s3, z4, cp, partial_sums = image_call(
            partial(leave_kernel, offset=c * steps), "leave", scalars, steps,
            [(act2[c], spec_rows(narrow)), *rim_in(rims2[c]), (fwd_two, spec_whole(fwd_two)),
             (bias_two, spec_whole(bias_two)), (hat_out, spec_whole(hat_out)),
             (bias_out, spec_whole(bias_out)), (cotangent, spec_slots(wide, c * steps))],
            [mid(), far(), big(), big(),
             (jax.ShapeDtypeStruct((steps * 16, 2 * wide // 3), F32),
              pl.BlockSpec((16, 2 * wide // 3), lambda j, *_: (j, 0)))],
            [tile_scratch, mask_scratch, flat_scratch], work + conv_work,
        )
        act3.append(a3), slope3.append(s3), four.append(z4), cotp.append(cp)
        sums.append(rows_sum(partial_sums))
    seh = squeeze_weight.shape[1]
    inputs = [*sums, squeeze_weight, squeeze_bias, excite_weight, excite_bias]
    rows = CHUNKS * steps * 8
    scale, shift, factors = pl.pallas_call(
        gate_kernel,
        in_specs=[pl.BlockSpec(memory_space=pltpu.VMEM)] * len(inputs)
        + [pl.BlockSpec(memory_space=pltpu.SMEM)],
        out_shape=[
            jax.ShapeDtypeStruct((rows, wide), F32),
            jax.ShapeDtypeStruct((rows, wide), F32),
            jax.ShapeDtypeStruct((rows, 2 * wide + 2 * seh + 128), BF),
        ],
        compiler_params=PARAMS,
        cost_estimate=SMALL,
        name="gate",
    )(*inputs, skip_gain)

    def rims_all(c):
        shape = jax.ShapeDtypeStruct((count * PITCH, narrow), BF)
        return (shape, spec_rows(narrow, c * steps, PITCH))

    grad4, grad3, edges = [], [], []
    for c in chunks:
        d4, d3, *edges = image_call(
            partial(turn_kernel, offset=c * steps), "turn", scalars, steps,
            [(cotp[c], spec_rows(wide)), (scale, spec_sums(wide, c * steps)), (shift, spec_sums(wide, c * steps)),
             (hat_out, spec_whole(hat_out)), (slope3[c], spec_rows(narrow)),
             *[(edge, pl.BlockSpec(memory_space=pl.ANY)) for edge in edges]],
            [big(), mid(), rims_all(c), rims_all(c)],
            [mask_scratch], work, [(5, 2), (6, 3)] if edges else [],
        )
        grad4.append(d4), grad3.append(d3)
    rims3 = neighbours(*edges)

    factors = lax.all_gather(factors, "batch", axis=0, tiled=True)

    def run_output(c, held):
        alias = [] if held is None else [(held, pl.BlockSpec(memory_space=pl.ANY))]
        (out,) = image_call(
            partial(output_kernel, offset=c * steps), "output", scalars, steps,
            [(images, spec_slots(wide, c * steps)), (four[c], spec_rows(wide)),
             (scale, spec_sums(wide, c * steps)), *alias],
            [(HBM(images.shape, BF), spec_slots(wide, c * steps))], [flat_scratch], 0,
            [(3, 0)] if alias else [],
        )
        return out

    def run_grad_images(c, held):
        alias = [] if held is None else [(held, pl.BlockSpec(memory_space=pl.ANY))]
        (out,) = image_call(
            partial(grad_image_kernel, offset=c * steps), "grad_images", scalars, steps,
            [(grad1[c], spec_rows(narrow)), (hat_in, spec_whole(hat_in)),
             (slope0[c], spec_rows(wide)), (cotp[c], spec_rows(wide)), *alias],
            [(HBM(images.shape, BF), spec_slots(wide, c * steps))],
            [pltpu.VMEM((STEP * ROWS_IMG, wide), F32), flat_scratch], work, [(4, 0)] if alias else [],
        )
        return out

    groups = []

    def slot(run, value, *landing, rims=()):
        for group in groups:
            value = group.hold(value)
        value = run(value)
        for group in landing:
            value = group.land(value)
            if group.landed:
                groups.remove(group)
        for group in landing:
            if not group.landed:
                rims, group.send = ordered(rims, group.send)
                group.fly()
        return (value, rims) if rims else value

    def start(*blocks):
        group = Reduction(*blocks)
        group.fly()
        groups.append(group)
        return group

    def rims_of(rims, c):
        return [(rim, spec_rows(narrow, c * steps, PITCH)) for rim in rims]

    def run_back_two(c, edges, values):
        grad, rims = values
        return image_call(
            partial(conv_back_kernel, offset=c * steps, edged=True), "back_two", scalars, steps,
            [(grad, spec_rows(narrow)), *rims_of(rims, c), (fwd_two, spec_whole(fwd_two)),
             (slope2[c], spec_rows(narrow)), *[(edge, pl.BlockSpec(memory_space=pl.ANY)) for edge in edges]],
            [mid(), rims_all(c), rims_all(c)],
            [tile_scratch], conv_work, [(5, 1), (6, 2)] if edges else [],
        )

    def run_back_one(values):
        grads, rims = values
        return [
            image_call(
                partial(conv_back_kernel, offset=c * steps, edged=False), "back_one", scalars, steps,
                [(grads[c], spec_rows(narrow)), *rims_of(rims, c), (fwd_one, spec_whole(fwd_one)),
                 (slope1[c], spec_rows(narrow))],
                [mid()],
                [tile_scratch], conv_work,
            )[0]
            for c in chunks
        ]

    *part_out, vec_out = weight_flat(core, act3, grad4, proj_out, stat_out, narrow, "weight_out")
    rims3, part_out = ordered(rims3, part_out)
    group_out = start(part_out)
    first, *edges = slot(lambda values: run_back_two(0, [], values), (grad3[0], rims3), group_out)
    second, *edges = slot(lambda values: run_back_two(1, values[2], values[:2]), (grad3[1], rims3, edges))
    grad2, rims4 = [first, second], neighbours(*edges)
    conv_two_args = (act2, rims2, grad3, conv_two, stat_two)
    conv_one_args = (act1, rims1, grad2, conv_one, stat_one)
    two = slot(lambda args: weight_conv(core, scalars, *args, "weight_two"), conv_two_args)
    *part_two, vec_two = group_out.land(two)
    one = weight_conv(core, scalars, *group_out.hold(conv_one_args), "weight_one")
    rims4, (one, group_out.send) = ordered(rims4, (one, group_out.send))
    *part_one, vec_one = one
    group_out.fly()
    group_conv = start(part_one, part_two)
    grad1 = slot(run_back_one, (grad2, rims4), group_out, group_conv)
    *part_in, vec_in = slot(
        lambda grads: weight_flat(core, act0, grads, proj_in, stat_in, narrow, "weight_in"), grad1, group_out, group_conv
    )
    group_conv.send, part_in = ordered(group_conv.send, part_in)
    half = jax.ShapeDtypeStruct((4, 16, narrow), BF)
    part_vec = small_call(
        vector_kernel, "vectors", [core], [vec_in, vec_one, vec_two, vec_out], [half, half]
    )
    group_in = start(part_in, part_vec)

    def run_output(c, four_rows, held):
        alias = [] if held is None else [(held, pl.BlockSpec(memory_space=pl.ANY))]
        return image_call(
            partial(output_kernel, offset=c * steps), "output", scalars, steps,
            [(images, spec_slots(wide, c * steps)), (four_rows, spec_rows(wide)),
             (scale, spec_sums(wide, c * steps)), *alias],
            [(HBM(images.shape, BF), spec_slots(wide, c * steps))], [flat_scratch], 0,
            [(3, 0)] if alias else [],
        )[0]

    def run_grad_images(c, grads, held):
        alias = [] if held is None else [(held, pl.BlockSpec(memory_space=pl.ANY))]
        return image_call(
            partial(grad_image_kernel, offset=c * steps), "grad_images", scalars, steps,
            [(grads, spec_rows(narrow)), (hat_in, spec_whole(hat_in)),
             (slope0[c], spec_rows(wide)), (cotp[c], spec_rows(wide)), *alias],
            [(HBM(images.shape, BF), spec_slots(wide, c * steps))],
            [pltpu.VMEM((STEP * ROWS_IMG, wide), F32), flat_scratch], work, [(4, 0)] if alias else [],
        )[0]

    def spread(group, *shapes, vectors=()):
        def run(got):
            group.got = got
            return group.spread(*shapes, vectors=vectors)

        return run

    flat_conv = (9 * GW, narrow)
    grad_images = slot(lambda grads: run_grad_images(0, grads, None), grad1[0], group_in, group_out)
    grad_images = slot(lambda held: run_grad_images(1, grad1[1], held), grad_images, group_conv, group_out)
    output = slot(lambda rows: run_output(0, rows, None), four[0], group_in)
    output = slot(lambda held: run_output(1, four[1], held), output, group_conv, group_out)
    grad_ex_w, grad_ex_b = slot(lambda f: outer(f, wide + seh, seh, wide, "outer_excite"), factors, group_in)
    squeeze = slot(lambda f: outer(f, 0, wide, seh, "outer_squeeze", skip=True), factors, group_conv, group_out)
    assert group_out.landed
    (sum_out,) = slot(spread(group_out, proj_out.shape), group_out.got, group_in)
    for landing in (group_conv, group_in, group_conv, group_in, group_conv):
        sum_out = slot(lambda value: value, sum_out, landing)
    assert group_conv.landed
    sum_one, sum_two = slot(spread(group_conv, flat_conv, flat_conv), group_conv.got, group_in)
    while groups:
        sum_one = slot(lambda value: value, sum_one, group_in)
    grad_sq_w, grad_sq_b, skip_table = squeeze
    vectors = [(narrow,)] * 6 + [(wide,)] * 2
    sum_in, *vec = group_in.spread(proj_in.shape, vectors=vectors)
    return (
        output.transpose(0, 2, 1, 3),
        grad_images.transpose(0, 2, 1, 3),
        sum_in,
        vec[0],
        vec[1],
        sum_one.reshape(conv_one.shape),
        vec[2],
        vec[3],
        sum_two.reshape(conv_two.shape),
        vec[4],
        vec[5],
        sum_out,
        vec[6],
        vec[7],
        grad_sq_w,
        grad_sq_b,
        grad_ex_w,
        grad_ex_b,
        skip_table[0, :1],
    )


def solution(mesh):
    slots = P("batch", "rows", None, None)
    return jax.shard_map(
        shards,
        mesh=mesh,
        in_specs=(slots, P("batch"), slots) + (P(),) * 17,
        out_specs=(slots, slots) + (P(),) * 17,
        check_vma=False,
    )
```

```python
from functools import partial

import jax
import jax.numpy as jnp
from jax import lax
from jax.experimental import pallas as pl
from jax.experimental.pallas import tpu as pltpu
from jax.sharding import PartitionSpec as P

GW = 128
ROW_SLOTS = 4
COL_SLOTS = 14
PITCH = 16
ROWS_IMG = ROW_SLOTS * PITCH
TILE_IMG = ROWS_IMG + 2 * PITCH
PIXELS = 140
STEP = 5
CHUNKS = 2

GAMMA = 1.7015043497
BETA_SCALE = 0.9128709291752769
ALPHA = 0.2
WS_EPS = 1e-05
ROOT_HALF = 0.7071067811865476
INV_ROOT_TWO_PI = 0.3989422804014327
BF = jnp.bfloat16
F32 = jnp.float32
NN = (((1,), (0,)), ((), ()))
NT = (((1,), (1,)), ((), ()))
TN = (((0,), (0,)), ((), ()))
HBM = pltpu.HBM
SMALL = pl.CostEstimate(flops=1, bytes_accessed=1, transcendentals=0)
PARAMS = pltpu.CompilerParams(vmem_limit_bytes=28 * 2**20)


def dot(left, right, dims=NN):
    return lax.dot_general(left, right, dims, preferred_element_type=F32)


def normal_parts(signal):
    phi = 0.5 + 0.5 * lax.erf(signal * ROOT_HALF)
    bell = jnp.exp(-0.5 * signal * signal) * INV_ROOT_TWO_PI
    return phi, bell


def gelu_and_slope(signal):
    phi, bell = normal_parts(signal)
    return (GAMMA * signal) * phi, GAMMA * (phi + signal * bell)


def at_row(index):
    return pl.ds(pl.multiple_of(index * PITCH, PITCH), PITCH)


def lanes(mask, width):
    return jnp.concatenate([mask] * (width // 128), axis=1)


def slot_width(counts, widths, image, slot):
    return jnp.where(slot < counts[image], widths[image], 0)


def below(limit, shape):
    return lax.broadcasted_iota(jnp.int32, shape, 0) < limit


def fill_mask(counts, widths, base, mask_ref):
    for image in range(STEP):
        for slot in range(ROW_SLOTS):
            limit = slot_width(counts, widths, base + image, slot)
            row = image * ROW_SLOTS + slot
            mask_ref[row * PITCH : (row + 1) * PITCH, :] = below(limit, (PITCH, 128)).astype(F32)


def lane_tiles(width):
    return [(tile, slice(tile * 128, (tile + 1) * 128)) for tile in range(width // 128)]


def unpack_image(slots_ref, image, flat_ref):
    for col in range(COL_SLOTS):
        value = slots_ref[image, col].astype(F32)
        for tile, span in lane_tiles(value.shape[1]):
            flat_ref[tile, col * ROW_SLOTS : (col + 1) * ROW_SLOTS, :] = value[:, span]


def pack_image(flat_ref, slots_ref, image):
    for col in range(COL_SLOTS):
        rows = slice(col * ROW_SLOTS, (col + 1) * ROW_SLOTS)
        value = [flat_ref[tile, rows, :] for tile in range(flat_ref.shape[0])]
        slots_ref[image, col] = jnp.concatenate(value, axis=1).astype(BF)


def read_slot(flat_ref, slot):
    rows = pl.ds(slot, PITCH, stride=ROW_SLOTS)
    return jnp.concatenate([flat_ref[tile, rows, :] for tile in range(flat_ref.shape[0])], axis=1)


def write_slot(flat_ref, slot, value):
    rows = pl.ds(slot, PITCH, stride=ROW_SLOTS)
    for tile, span in lane_tiles(value.shape[1]):
        flat_ref[tile, rows, :] = value[:, span]


def clear_tail(flat_ref):
    first = ROW_SLOTS * COL_SLOTS
    flat_ref[:, first:, :] = jnp.zeros((flat_ref.shape[0], ROWS_IMG - first, 128), F32)


def store_edges(scalars, base, act_ref, even_ref, odd_ref):
    counts, _, place = scalars
    odd = place[0] == 1
    for image in range(STEP):
        dest = slice(image * PITCH, (image + 1) * PITCH)
        first = act_ref[image * ROWS_IMG : image * ROWS_IMG + PITCH, :]
        last = act_ref[at_row(image * ROW_SLOTS + counts[base + image] - 1), :]
        even_ref[dest, :] = jnp.where(odd, first, last)
        odd_ref[dest, :] = jnp.where(odd, last, first)


def fill_tile(scalars, base, act_ref, even_ref, odd_ref, tile_ref):
    counts, _, place = scalars
    odd = place[0] == 1
    tile_rows = TILE_IMG // PITCH
    for image in range(act_ref.shape[0] // ROWS_IMG):
        start = image * TILE_IMG
        rim = slice(image * PITCH, (image + 1) * PITCH)
        even, other = even_ref[rim, :], odd_ref[rim, :]
        tile_ref[start : start + PITCH, :] = jnp.where(odd, even, other)
        tile_ref[start + PITCH : start + PITCH + ROWS_IMG, :] = act_ref[
            image * ROWS_IMG : (image + 1) * ROWS_IMG, :
        ]
        tile_ref[start + PITCH + ROWS_IMG : start + TILE_IMG, :] = jnp.zeros(
            (PITCH, act_ref.shape[1]), act_ref.dtype
        )
        tile_ref[at_row(image * tile_rows + counts[base + image] + 1), :] = jnp.where(odd, other, even)


def group_cat(tile_ref, images, group):
    cols = slice(group * GW, (group + 1) * GW)
    return jnp.concatenate(
        [
            jnp.concatenate(
                [
                    tile_ref[
                        image * TILE_IMG + shift * PITCH : image * TILE_IMG + shift * PITCH + ROWS_IMG,
                        cols,
                    ]
                    for image in range(images)
                ],
                axis=0,
            )
            for shift in range(3)
        ],
        axis=1,
    )


def conv_group(tile_ref, images, group, weight, dims):
    wide = dot(group_cat(tile_ref, images, group), weight, dims)
    rows = wide.shape[0]
    return (
        wide[:, GW : 2 * GW]
        + pltpu.roll(wide[:, :GW], 1, 0)
        + pltpu.roll(wide[:, 2 * GW :], rows - 1, 0)
    )


def prep_flat_kernel(weight_ref, gain_ref, hat_ref, stat_ref):
    weight = weight_ref[...].astype(F32)
    fan = weight.shape[0]
    mean = jnp.sum(weight, axis=0, keepdims=True) * (1.0 / fan)
    center = weight - mean
    spread = jnp.sum(center * center, axis=0, keepdims=True) * (1.0 / fan)
    inv = lax.rsqrt(spread * fan + WS_EPS)
    gain = gain_ref[...][None, :]
    hat_ref[...] = (gain * center * inv).astype(BF)
    stat_ref[0:1, :] = mean
    stat_ref[1:2, :] = inv
    stat_ref[2:3, :] = gain


def prep_flat(weight, gain):
    fan, width = weight.shape
    block = 256
    return pl.pallas_call(
        prep_flat_kernel,
        grid=(width // block,),
        in_specs=[
            pl.BlockSpec((fan, block), lambda j: (0, j)),
            pl.BlockSpec((block,), lambda j: (j,)),
        ],
        out_specs=[
            pl.BlockSpec((fan, block), lambda j: (0, j)),
            pl.BlockSpec((8, block), lambda j: (0, j)),
        ],
        out_shape=[
            jax.ShapeDtypeStruct((fan, width), BF),
            jax.ShapeDtypeStruct((8, width), F32),
        ],
        compiler_params=PARAMS,
        name="prep_flat",
    )(weight, gain)


def prep_conv_kernel(weight_ref, gain_ref, fwd_ref, stat_ref):
    weight = weight_ref[...].astype(F32)
    fan = 9 * GW
    mean = jnp.sum(jnp.sum(weight, axis=0), axis=0, keepdims=True) * (1.0 / fan)
    center = weight - mean
    spread = jnp.sum(jnp.sum(center * center, axis=0), axis=0, keepdims=True) * (1.0 / fan)
    inv = lax.rsqrt(spread * fan + WS_EPS)
    gain = gain_ref[...][None, :]
    hat = (gain * center * inv).astype(BF)
    for row in range(3):
        for col in range(3):
            rows, cols = slice(row * GW, (row + 1) * GW), slice(col * GW, (col + 1) * GW)
            fwd_ref[0, rows, cols] = hat[3 * row + col]
    stat_ref[0:1, :] = mean
    stat_ref[1:2, :] = inv
    stat_ref[2:3, :] = gain


def prep_conv(weight, gain):
    width = weight.shape[2]
    groups = width // GW
    square = pl.BlockSpec((1, 3 * GW, 3 * GW), lambda j: (j, 0, 0))
    return pl.pallas_call(
        prep_conv_kernel,
        grid=(groups,),
        in_specs=[
            pl.BlockSpec((9, GW, GW), lambda j: (0, 0, j)),
            pl.BlockSpec((GW,), lambda j: (j,)),
        ],
        out_specs=[square, pl.BlockSpec((8, GW), lambda j: (0, j))],
        out_shape=[
            jax.ShapeDtypeStruct((groups, 3 * GW, 3 * GW), BF),
            jax.ShapeDtypeStruct((8, width), F32),
        ],
        compiler_params=PARAMS,
        name="prep_conv",
    )(weight, gain)


def spec_rows(width, offset=0, per=ROWS_IMG):
    return pl.BlockSpec((STEP * per, width), lambda j, *_: (j + offset, 0))


def spec_slots(width, offset):
    return pl.BlockSpec((STEP, COL_SLOTS, ROW_SLOTS, width), lambda j, *_: (j + offset, 0, 0, 0))


def spec_whole(array):
    zeros = (0,) * array.ndim
    return pl.BlockSpec(array.shape, lambda j, *_: zeros)


def spec_sums(width, offset):
    return pl.BlockSpec((8, width), lambda j, *_: (j + offset, 0))


def image_call(kernel, name, scalars, steps, inputs, outputs, scratch=(), flops=0, alias=()):
    return pl.pallas_call(
        kernel,
        grid_spec=pltpu.PrefetchScalarGridSpec(
            num_scalar_prefetch=len(scalars),
            grid=(steps,),
            in_specs=[spec for _, spec in inputs],
            out_specs=[spec for _, spec in outputs],
            scratch_shapes=list(scratch),
        ),
        out_shape=[shape for shape, _ in outputs],
        input_output_aliases={len(scalars) + source: target for source, target in alias},
        compiler_params=PARAMS,
        cost_estimate=SMALL,
        name=name,
    )(*scalars, *[array for array, _ in inputs])


def rows_out(steps, width, per=ROWS_IMG, dtype=BF, space=jax.ShapeDtypeStruct):
    return (space((steps * STEP * per, width), dtype), spec_rows(width, 0, per))


def enter_kernel(
    counts, widths, place, image_ref, hat_ref, bias_ref,
    act0_ref, slope0_ref, act1_ref, slope1_ref, even_ref, odd_ref, mask_ref, flat_ref, *, offset,
):
    base = (pl.program_id(0) + offset) * STEP
    fill_mask(counts, widths, base, mask_ref)
    clear_tail(flat_ref)

    def one_image(image, carry):
        unpack_image(image_ref, image, flat_ref)
        for slot in range(ROW_SLOTS):
            value = read_slot(flat_ref, slot)
            keep = below(slot_width(counts, widths, base + image, slot), value.shape)
            value = jnp.where(keep, value, 0.0)
            act, slope = gelu_and_slope(value)
            row = at_row(image * ROW_SLOTS + slot)
            act0_ref[row, :] = (act * BETA_SCALE).astype(BF)
            slope0_ref[row, :] = (slope * BETA_SCALE).astype(BF)
        return carry

    lax.fori_loop(0, STEP, one_image, 0)
    width = act1_ref.shape[1]
    block = 256
    keep = lanes(mask_ref[...], block)
    for start in range(0, width, block):
        cols = slice(start, start + block)
        pre = dot(act0_ref[...], hat_ref[:, cols]) + bias_ref[cols][None, :]
        act, slope = gelu_and_slope(pre)
        act1_ref[:, cols] = (act * keep).astype(BF)
        slope1_ref[:, cols] = (slope * keep).astype(BF)
    store_edges((counts, widths, place), base, act1_ref, even_ref, odd_ref)


def conv_body(tile_ref, weight_ref, bias_ref, out_ref, slope_ref, keep):
    for group in range(weight_ref.shape[0]):
        cols = slice(group * GW, (group + 1) * GW)
        pre = conv_group(tile_ref, STEP, group, weight_ref[group], NN) + bias_ref[cols][None, :]
        act, slope = gelu_and_slope(pre)
        out_ref[:, cols] = (act * keep).astype(BF)
        slope_ref[:, cols] = (slope * keep).astype(BF)


def conv_kernel(
    counts, widths, place, act_ref, up_ref, down_ref, weight_ref, bias_ref,
    out_ref, slope_ref, even_ref, odd_ref, tile_ref, mask_ref, *, offset,
):
    base = (pl.program_id(0) + offset) * STEP
    scalars = (counts, widths, place)
    fill_mask(counts, widths, base, mask_ref)
    fill_tile(scalars, base, act_ref, up_ref, down_ref, tile_ref)
    conv_body(tile_ref, weight_ref, bias_ref, out_ref, slope_ref, mask_ref[...])
    store_edges(scalars, base, out_ref, even_ref, odd_ref)


def leave_kernel(
    counts, widths, place, act_ref, up_ref, down_ref, weight_ref, bias_ref, hat_ref, bias_out_ref, cot_ref,
    out_ref, slope_ref, four_ref, cotp_ref, sum_ref, tile_ref, mask_ref, flat_ref, *, offset,
):
    base = (pl.program_id(0) + offset) * STEP
    fill_mask(counts, widths, base, mask_ref)
    fill_tile((counts, widths, place), base, act_ref, up_ref, down_ref, tile_ref)
    clear_tail(flat_ref)

    def one_image(image, carry):
        unpack_image(cot_ref, image, flat_ref)
        for slot in range(ROW_SLOTS):
            value = read_slot(flat_ref, slot)
            keep = below(slot_width(counts, widths, base + image, slot), value.shape)
            cotp_ref[at_row(image * ROW_SLOTS + slot), :] = jnp.where(keep, value, 0.0).astype(BF)
        return carry

    lax.fori_loop(0, STEP, one_image, 0)
    keep = mask_ref[...]
    conv_body(tile_ref, weight_ref, bias_ref, out_ref, slope_ref, keep)
    width = four_ref.shape[1]
    block = 256
    keep = lanes(keep, block)
    sum_ref[...] = jnp.zeros_like(sum_ref)
    third = sum_ref.shape[1]

    def put(values, image, column):
        row = column // third * STEP + image
        sum_ref[row : row + 1, column % third : column % third + block] = jnp.sum(
            values[image * ROWS_IMG : (image + 1) * ROWS_IMG], axis=0, keepdims=True
        )

    for start in range(0, width, block):
        cols = slice(start, start + block)
        pre = dot(out_ref[...], hat_ref[:, cols]) + bias_out_ref[cols][None, :]
        four_ref[:, cols] = pre.astype(BF)
        held = pre * keep
        cross = pre * cotp_ref[:, cols].astype(F32)
        for image in range(STEP):
            put(held, image, start)
            put(cross, image, width + start)


def unpacked_sums(*sum_refs):
    rows = []
    for sum_ref in sum_refs:
        for step in range(0, sum_ref.shape[0], 16):
            thirds = [sum_ref[step + STEP * t : step + STEP * (t + 1), :] for t in range(3)]
            rows.append(jnp.concatenate(thirds, axis=1))
            rows.append(jnp.zeros((8 - STEP, 3 * sum_ref.shape[1]), F32))
    return jnp.concatenate(rows, axis=0)


def two_pass(left, right, dims=NN):
    high = left.astype(BF)
    low = (left - high.astype(F32)).astype(BF)
    both = dot(jnp.concatenate([high, low], axis=0), right, dims)
    return both[: left.shape[0]] + both[left.shape[0] :]


def gate_kernel(
    sum0_ref, sum1_ref, squeeze_ref, squeeze_bias_ref, excite_ref, excite_bias_ref, skip_ref,
    scale_ref, shift_ref, factor_ref,
):
    width = scale_ref.shape[1]
    skip = skip_ref[0]
    sums = unpacked_sums(sum0_ref, sum1_ref)
    pooled = sums[:, :width] * (1.0 / PIXELS)
    cross = sums[:, width:] * ALPHA
    squeezed = two_pass(pooled, squeeze_ref[...]) + squeeze_bias_ref[...][None, :]
    phi, bell = normal_parts(squeezed)
    hidden = squeezed * phi
    excited = two_pass(hidden, excite_ref[...]) + excite_bias_ref[...][None, :]
    gate = 2.0 * jax.nn.sigmoid(excited)
    dexcite = (cross * skip) * gate * (1.0 - 0.5 * gate)
    dsqueeze = two_pass(dexcite, excite_ref[...], NT) * (phi + squeezed * bell)
    scale_ref[...] = (ALPHA * skip) * gate
    shift_ref[...] = two_pass(dsqueeze, squeeze_ref[...], NT) * (1.0 / PIXELS)
    dskip = jnp.sum(gate * cross, axis=1, keepdims=True)
    high = dskip.astype(BF).astype(F32)
    mid = (dskip - high).astype(BF).astype(F32)
    lane = lax.broadcasted_iota(jnp.int32, (dskip.shape[0], 128), 1)
    pieces = jnp.where(lane == 0, high, jnp.where(lane == 1, mid, dskip - high - mid))
    pieces = jnp.where(lane < 3, pieces, 0.0)
    factor_ref[...] = jnp.concatenate([pooled, dsqueeze, hidden, dexcite, pieces], axis=1).astype(BF)


def turn_kernel(
    counts, widths, place, cotp_ref, scale_ref, shift_ref, hat_ref, slope_ref, *rest, offset
):
    four_ref, three_ref, even_ref, odd_ref, mask_ref = rest[-5:]
    base = (pl.program_id(0) + offset) * STEP
    fill_mask(counts, widths, base, mask_ref)
    for image in range(STEP):
        rows = slice(image * ROWS_IMG, (image + 1) * ROWS_IMG)
        keep = lanes(mask_ref[rows, :], four_ref.shape[1])
        value = cotp_ref[rows, :].astype(F32) * scale_ref[image : image + 1, :]
        value = value + keep * shift_ref[image : image + 1, :]
        four_ref[rows, :] = value.astype(BF)
    width = three_ref.shape[1]
    block = 256
    for start in range(0, width, block):
        cols = slice(start, start + block)
        back = dot(four_ref[...], hat_ref[cols, :], NT)
        three_ref[:, cols] = (back * slope_ref[:, cols].astype(F32)).astype(BF)
    store_edges((counts, widths, place), base, three_ref, even_ref, odd_ref)


def turned(weight_ref, group):
    square = lambda row, col: weight_ref[
        group, (2 - row) * GW : (3 - row) * GW, (2 - col) * GW : (3 - col) * GW
    ]
    return jnp.concatenate(
        [jnp.concatenate([square(row, col) for row in range(3)], axis=1) for col in range(3)], axis=0
    )


def conv_back_kernel(
    counts, widths, place, grad_ref, up_ref, down_ref, weight_ref, slope_ref, *rest, offset, edged
):
    out_ref, *edges, tile_ref = rest[-4:] if edged else rest
    base = (pl.program_id(0) + offset) * STEP
    scalars = (counts, widths, place)
    fill_tile(scalars, base, grad_ref, up_ref, down_ref, tile_ref)
    for group in range(weight_ref.shape[0]):
        cols = slice(group * GW, (group + 1) * GW)
        back = conv_group(tile_ref, STEP, group, turned(weight_ref, group), NT)
        out_ref[:, cols] = (back * slope_ref[:, cols].astype(F32)).astype(BF)
    if edges:
        store_edges(scalars, base, out_ref, *edges)


def grad_image_kernel(counts, widths, place, grad_ref, hat_ref, slope_ref, cotp_ref, *rest, offset):
    out_ref, work_ref, flat_ref = rest[-3:]
    base = (pl.program_id(0) + offset) * STEP
    width = hat_ref.shape[0]
    block = 256
    for start in range(0, width, block):
        cols = slice(start, start + block)
        back = dot(grad_ref[...], hat_ref[cols, :], NT)
        work_ref[:, cols] = back * slope_ref[:, cols].astype(F32) + cotp_ref[:, cols].astype(F32)

    def one_image(image, carry):
        for slot in range(ROW_SLOTS):
            value = work_ref[at_row(image * ROW_SLOTS + slot), :]
            keep = below(slot_width(counts, widths, base + image, slot), value.shape)
            write_slot(flat_ref, slot, jnp.where(keep, value, 0.0))
        pack_image(flat_ref, out_ref, image)
        return carry

    lax.fori_loop(0, STEP, one_image, 0)


def output_kernel(counts, widths, place, image_ref, four_ref, scale_ref, *rest, offset):
    out_ref, flat_ref = rest[-2:]
    base = (pl.program_id(0) + offset) * STEP
    clear_tail(flat_ref)

    def one_image(image, carry):
        unpack_image(image_ref, image, flat_ref)
        for slot in range(ROW_SLOTS):
            value = read_slot(flat_ref, slot)
            four = four_ref[at_row(image * ROW_SLOTS + slot), :].astype(F32)
            keep = below(slot_width(counts, widths, base + image, slot), value.shape)
            value = jnp.where(keep, value + four * scale_ref[pl.ds(image, 1), :], 0.0)
            write_slot(flat_ref, slot, value)
        pack_image(flat_ref, out_ref, image)
        return carry

    lax.fori_loop(0, STEP, one_image, 0)


def split_halves(scratch_ref, core, keep_ref, send_ref):
    keep_ref[...] = scratch_ref[core]
    send_ref[...] = scratch_ref[1 - core]


def weight_flat_kernel(
    core, left0, left1, right0, right1, weight_ref, stat_ref, keep_ref, send_ref, vec_ref, scratch_ref
):
    pieces, rows, span = keep_ref.shape

    def store(start, grad):
        for first in range(0, grad.shape[0], rows):
            half, piece = divmod((start // span * grad.shape[0] + first) // rows, pieces)
            scratch_ref[half, piece, :, start % span : start % span + grad.shape[1]] = grad[
                first : first + rows
            ]

    weight_flat_body(left0, left1, right0, right1, weight_ref, stat_ref, store, vec_ref)
    split_halves(scratch_ref, core[0], keep_ref, send_ref)


def weight_flat_body(left0, left1, right0, right1, weight_ref, stat_ref, store, vec_ref):
    fan, width = weight_ref.shape
    block = 256
    vec_ref[...] = jnp.zeros_like(vec_ref)
    for start in range(0, width, block):
        cols = slice(start, start + block)
        ghat = dot(left0[...], right0[:, cols], TN) + dot(left1[...], right1[:, cols], TN)
        mean, inv, gain = stat_ref[0:1, cols], stat_ref[1:2, cols], stat_ref[2:3, cols]
        center = weight_ref[:, cols].astype(F32) - mean
        along = jnp.sum(ghat * center, axis=0, keepdims=True)
        level = jnp.sum(ghat, axis=0, keepdims=True) * (1.0 / fan)
        grad = ((gain * inv) * (ghat - level - center * (inv * inv * along))).astype(BF)
        store(start, grad)
        total = jnp.sum(right0[:, cols].astype(F32), axis=0, keepdims=True)
        total = total + jnp.sum(right1[:, cols].astype(F32), axis=0, keepdims=True)
        vec_ref[0:1, cols] = total
        vec_ref[1:2, cols] = inv * along


def halves_out(rows, span):
    shape = (4, rows // 8, span)
    return [jax.ShapeDtypeStruct(shape, BF)] * 2, pltpu.VMEM((2, *shape), BF)


def weight_call(kernel, name, scalars, inputs, rows, span, width, scratch, flops):
    halves, both = halves_out(rows, span)
    return pl.pallas_call(
        kernel,
        in_specs=[pl.BlockSpec(memory_space=pltpu.SMEM)] * len(scalars)
        + [pl.BlockSpec(memory_space=pltpu.VMEM)] * len(inputs),
        out_shape=[*halves, jax.ShapeDtypeStruct((8, width), F32)],
        scratch_shapes=[both, *scratch],
        compiler_params=PARAMS,
        cost_estimate=SMALL,
        name=name,
    )(*scalars, *inputs)


def weight_flat(core, lefts, rights, weight, stat, span, name):
    fan, width = weight.shape
    return weight_call(
        weight_flat_kernel, name, [core], [*lefts, *rights, weight, stat],
        fan * width // span, span, width, [], 4 * fan * width * lefts[0].shape[0],
    )


def weight_conv_kernel(
    core, counts, widths, place, act0, act1, even0, even1, odd0, odd1, grad0, grad1, weight_ref, stat_ref,
    keep_ref, send_ref, vec_ref, scratch_ref, tile_ref,
):
    images = act0.shape[0] // ROWS_IMG
    fan = 9 * GW
    scalars = (counts, widths, place)
    pieces, piece_rows, _ = keep_ref.shape
    fill_tile(scalars, 0, act0, even0, odd0, tile_ref.at[0])
    fill_tile(scalars, images, act1, even1, odd1, tile_ref.at[1])
    vec_ref[...] = jnp.zeros_like(vec_ref)
    for group in range(weight_ref.shape[2] // GW):
        cols = slice(group * GW, (group + 1) * GW)
        ghat = jnp.zeros((3 * GW, 3 * GW), F32)
        total = jnp.zeros((1, GW), F32)
        for index, grad_ref in enumerate((grad0, grad1)):
            grad = grad_ref[:, cols].astype(F32)
            rows = grad.shape[0]
            total = total + jnp.sum(grad, axis=0, keepdims=True)
            wide = jnp.concatenate(
                [
                    pltpu.roll(grad, rows - 1, 0).astype(BF),
                    grad_ref[:, cols],
                    pltpu.roll(grad, 1, 0).astype(BF),
                ],
                axis=1,
            )
            ghat = ghat + dot(group_cat(tile_ref.at[index], images, group), wide, TN)
        mean, inv, gain = stat_ref[0:1, cols], stat_ref[1:2, cols], stat_ref[2:3, cols]
        along = jnp.zeros((1, GW), F32)
        level = jnp.zeros((1, GW), F32)
        centers, taps = [], []
        for tap in range(9):
            row, col = tap // 3, tap % 3
            part = ghat[row * GW : (row + 1) * GW, col * GW : (col + 1) * GW]
            center = weight_ref[tap, :, cols].astype(F32) - mean
            along = along + jnp.sum(part * center, axis=0, keepdims=True)
            level = level + jnp.sum(part, axis=0, keepdims=True)
            centers.append(center)
            taps.append(part)
        level = level * (1.0 / fan)
        slope = inv * inv * along
        for tap in range(9):
            grad = ((gain * inv) * (taps[tap] - level - centers[tap] * slope)).astype(BF)
            row = 0
            while row < GW:
                whole, inside = divmod(tap * GW + row, piece_rows)
                half, piece = divmod(whole, pieces)
                size = min(piece_rows - inside, GW - row)
                scratch_ref[half, piece, inside : inside + size, cols] = grad[row : row + size]
                row += size
        vec_ref[0:1, cols] = total
        vec_ref[1:2, cols] = inv * along
    split_halves(scratch_ref, core[0], keep_ref, send_ref)


def weight_conv(core, scalars, acts, rims, grads, weight, stat, name):
    width = weight.shape[2]
    images = acts[0].shape[0] // ROWS_IMG
    inputs = [*acts, *[r[0] for r in rims], *[r[1] for r in rims], *grads, weight, stat]
    return weight_call(
        weight_conv_kernel, name, [core, *scalars], inputs, 9 * GW, width, width,
        [pltpu.VMEM((2, images * TILE_IMG, width), BF)], 36 * GW * width * acts[0].shape[0],
    )


def outer_kernel(factor_ref, out_ref, sum_ref, *skip, start):
    left, right = out_ref.shape
    factor = factor_ref[:, start + left : start + left + right]
    out_ref[...] = dot(factor_ref[:, start : start + left], factor, TN)
    sum_ref[...] = jnp.sum(factor.astype(F32), axis=0)
    for ref in skip:
        pieces = factor_ref[:, factor_ref.shape[1] - 128 :].astype(F32)
        ref[...] = jnp.broadcast_to(jnp.sum(pieces), ref.shape)


def outer(factors, start, left, right, name, skip=False):
    return pl.pallas_call(
        partial(outer_kernel, start=start),
        out_shape=[HBM((left, right), F32), jax.ShapeDtypeStruct((right,), F32)]
        + [jax.ShapeDtypeStruct((8, 128), F32)] * skip,
        compiler_params=PARAMS,
        cost_estimate=SMALL,
        name=name,
    )(factors)


def vector_kernel(core, in_ref, one_ref, two_ref, out_ref, keep_ref, send_ref):
    span = keep_ref.shape[2]
    keep_ref[...] = jnp.zeros_like(keep_ref)
    send_ref[...] = jnp.zeros_like(send_ref)
    rows = [ref[r : r + 1, :] for ref in (in_ref, one_ref, two_ref) for r in range(2)]
    rows += [out_ref[r : r + 1, c : c + span] for r in range(2) for c in range(0, out_ref.shape[1], span)]
    rows.append(jnp.zeros((16 - len(rows), span), F32))
    block = jnp.concatenate(rows, axis=0)
    keep_ref[0] = jnp.where(core[0] == 0, block, 0.0).astype(BF)
    send_ref[0] = jnp.where(core[0] == 0, 0.0, block).astype(BF)


def swap(block, axis, bit):
    count = lax.axis_size(axis)
    return lax.ppermute(block, axis, [(i, i ^ (1 << bit)) for i in range(count)])


def bit_of(axis, bit):
    return ((lax.axis_index(axis) >> bit) & 1).astype(jnp.int32)


def neighbours(even, odd):
    count = lax.axis_size("rows")
    inner = [(i, i + 1) for i in range(1, count - 1, 2)]
    outer_pairs = [(i, i + 1) for i in range(0, count, 2)]
    both = lambda pairs: pairs + [(target, source) for source, target in pairs]
    return lax.ppermute(even, "rows", both(outer_pairs)), lax.ppermute(odd, "rows", both(inner))


def rows_sum(total):
    for bit in range(lax.axis_size("rows").bit_length() - 1):
        total = total + swap(total, "rows", bit)
    return total


def orders():
    bits = lax.axis_size("batch").bit_length() - 1
    middle = 1 + (bits - 1) // 2
    along_x = [("batch", bit) for bit in range(1, middle)]
    along_y = [("batch", bit) for bit in range(middle, bits)]
    along_z = [("rows", bit) for bit in range(lax.axis_size("rows").bit_length() - 1)]
    return [along_x + along_y + along_z, along_y + along_z + along_x]


def swap_way(block, ways, step):
    rows = lax.axis_size("rows")
    pairs = []
    for index in range(lax.axis_size("batch") * rows):
        axis, bit = ways[(index // rows) & 1][step]
        pairs.append((index, index ^ ((rows if axis == "batch" else 1) << bit)))
    return lax.ppermute(block, ("batch", "rows"), pairs)


def small_call(kernel, name, scalars, inputs, outputs):
    return pl.pallas_call(
        kernel,
        in_specs=[pl.BlockSpec(memory_space=pltpu.SMEM)] * len(scalars)
        + [pl.BlockSpec(memory_space=pltpu.VMEM)] * len(inputs),
        out_shape=outputs,
        compiler_params=PARAMS,
        cost_estimate=SMALL,
        name=name,
    )(*scalars, *inputs)


def first_kernel(bits, *refs):
    sources, (kept, send) = refs[:-2], refs[-2:]
    mine = bits[0]
    for second in range(2):
        for index, dest in ((2 * mine + second, kept), (2 * (1 - mine) + second, send)):
            row = 0
            for keep, got in zip(sources[0::2], sources[1::2]):
                rows = keep.shape[1]
                value = keep[index].astype(F32) + got[index].astype(F32)
                dest[second, row : row + rows, :] = value.astype(dest.dtype)
                row += rows


def second_kernel(bits, kept, got, keep, send):
    mine = bits[1]
    keep[...] = kept[mine] + got[mine].astype(F32)
    send[...] = (kept[1 - mine] + got[1 - mine].astype(F32)).astype(BF)


def add_kernel(left, right, out):
    out[...] = (left[...].astype(F32) + right[...].astype(F32)).astype(BF)


def pair_kernel(left, right, out):
    out[0] = left[...]
    out[1] = right[...]


def join_kernel(left, right, out):
    out[0:2] = left[...]
    out[2:4] = right[...]


def spread_kernel(bits, own_ref, other_ref, *outs, vectors):
    pieces, _, span = own_ref.shape
    core = bits[2]
    if vectors:
        outs, lines, table = outs[: -1 - vectors], outs[-1 - vectors : -1], outs[-1]
        outs = [*outs, table]
    for piece in range(pieces):
        place = 2 * (bits[0] ^ (piece >> 1)) + (bits[1] ^ (piece & 1))
        other_place = 2 * (bits[3] ^ (piece >> 1)) + (bits[4] ^ (piece & 1))
        row = 0
        for out in outs:
            rows = out.shape[0] * out.shape[1] // (2 * pieces * span)
            if out.shape[1] == span:
                for half, where, ref in ((core, place, own_ref), (1 - core, other_place, other_ref)):
                    at = pl.ds(pl.multiple_of((half * pieces + where) * rows, rows), rows)
                    out[at, :] = ref[piece, row : row + rows].astype(F32)
            else:
                for half in range(2):

                    @pl.when(core == half)
                    def _(half=half, row=row, out=out, rows=rows):
                        for side, where, ref in ((half, place, own_ref), (1 - half, other_place, other_ref)):
                            at = pl.ds(pl.multiple_of(where * rows, rows), rows)
                            out[at, side * span : (side + 1) * span] = ref[piece, row : row + rows].astype(F32)

            row += rows
    if vectors:
        row = 0
        for out in lines:
            for start in range(0, out.shape[0], span):
                out[start : start + span] = table[row]
                row += 1


def interleave(left, right):
    return [item for pair in zip(left, right) for item in pair]


def ordered(before, after):
    flat_before, tree_before = jax.tree.flatten(before)
    flat_after, tree_after = jax.tree.flatten(after)
    out = lax.optimization_barrier((*flat_before, *flat_after))
    split = len(flat_before)
    return tree_before.unflatten(out[:split]), tree_after.unflatten(out[split:])


class Reduction:
    def __init__(self, *blocks):
        self.landed = False
        self.keep = [keep for keep, _ in blocks]
        self.send = [send for _, send in blocks]
        self.rows = [keep.shape[1] for keep in self.keep]
        rows, span = sum(self.rows), self.keep[0].shape[2]
        self.shape = lambda dtype, *lead: jax.ShapeDtypeStruct((*lead, rows, span), dtype)
        ways = orders()
        core = bit_of("batch", 0)
        mine = [[bit_of(*way[step]) for step in range(2)] for way in ways]
        choose = lambda step, which: jnp.where(core == which, mine[0][step], mine[1][step])
        self.bits = jnp.stack([choose(0, 0), choose(1, 0), core, choose(0, 1), choose(1, 1)])
        across = lambda step: lambda blocks: [swap_way(block, ways, step) for block in blocks]
        chip = lambda blocks: [swap(block, "batch", 0) for block in blocks]
        self.plan = [(chip, self.halve_first), (across(0), self.halve_second), (across(1), self.add_last)]
        self.plan += [(across(step), self.add_all) for step in (2, 3)]
        self.across, self.rest = across, range(4, len(ways[0]))
        self.plan += [(across(1), self.pair), (across(0), self.join), (chip, self.done)]

    def fly(self):
        self.move, self.work = self.plan.pop(0)
        self.got = self.move(self.send)

    def land(self, before):
        before, (self.keep, self.got) = ordered(before, (self.keep, self.got))
        self.work()
        return before

    def hold(self, after):
        self.send, after = ordered(self.send, after)
        return after

    def call(self, kernel, name, bits, left, right, outputs):
        return small_call(kernel, name, bits, interleave(left, right), outputs)

    def halve_first(self):
        outs = [self.shape(F32, 2), self.shape(BF, 2)]
        kept, send = self.call(first_kernel, "halve_first", [self.bits], self.keep, self.got, outs)
        self.keep, self.send = [kept], [send]

    def halve_second(self):
        outs = [self.shape(F32), self.shape(BF)]
        kept, send = self.call(second_kernel, "halve_second", [self.bits], self.keep, self.got, outs)
        self.keep, self.send = [kept], [send]

    def add_last(self):
        self.send = self.call(add_kernel, "add_last", [], self.keep, self.got, [self.shape(BF)])
        self.keep = []

    def add_all(self):
        self.send = self.call(add_kernel, "add_all", [], self.send, self.got, [self.shape(BF)])
        if self.plan[0][1] == self.pair:
            for step in self.rest:
                got = self.across(step)(self.send)
                self.send = self.call(add_kernel, "add_all", [], self.send, got, [self.shape(BF)])

    def pair(self):
        self.send = self.call(pair_kernel, "pair", [], self.send, self.got, [self.shape(BF, 2)])

    def join(self):
        self.send = self.call(join_kernel, "join", [], self.send, self.got, [self.shape(BF, 4)])

    def done(self):
        self.landed = True

    def spread(self, *shapes, vectors=()):
        inputs = [self.send[0], self.got[0]]
        return pl.pallas_call(
            partial(spread_kernel, vectors=len(vectors)),
            in_specs=[pl.BlockSpec(memory_space=pltpu.SMEM)] + [pl.BlockSpec(memory_space=pltpu.VMEM)] * 2,
            out_shape=[HBM(shape, F32) for shape in shapes]
            + [jax.ShapeDtypeStruct(shape, F32) for shape in vectors],
            scratch_shapes=[pltpu.VMEM((128, inputs[0].shape[2]), F32)] if vectors else [],
            compiler_params=PARAMS,
            cost_estimate=SMALL,
            name="spread",
        )(self.bits, *inputs)


def shards(
    images, orientation, cotangent, proj_in, bias_in, gain_in, conv_one, bias_one, gain_one,
    conv_two, bias_two, gain_two, proj_out, bias_out, gain_out, squeeze_weight, squeeze_bias,
    excite_weight, excite_bias, skip_gain,
):
    count = images.shape[0]
    wide, narrow = proj_in.shape
    steps = count // STEP // CHUNKS
    images = images.transpose(0, 2, 1, 3)
    cotangent = cotangent.transpose(0, 2, 1, 3)
    height = jnp.where(orientation == 0, 10, 14).astype(jnp.int32)
    widths = 24 - height
    row_index = lax.axis_index("rows")
    counts = height // 4 + (row_index < height % 4).astype(jnp.int32)
    core = bit_of("batch", 0).reshape(1)
    scalars = (counts, widths, (row_index % 2).astype(jnp.int32).reshape(1))
    mask_scratch = pltpu.VMEM((STEP * ROWS_IMG, 128), F32)
    tile_scratch = pltpu.VMEM((STEP * TILE_IMG, narrow), BF)
    flat_scratch = pltpu.VMEM((wide // 128, ROWS_IMG, 128), F32)
    work = 2 * steps * STEP * ROWS_IMG * wide * narrow
    conv_work = 2 * steps * STEP * ROWS_IMG * 12 * GW * narrow

    hat_in, stat_in = prep_flat(proj_in, gain_in)
    fwd_one, stat_one = prep_conv(conv_one, gain_one)
    fwd_two, stat_two = prep_conv(conv_two, gain_two)
    hat_out, stat_out = prep_flat(proj_out, gain_out)

    chunks = range(CHUNKS)
    rim = lambda: rows_out(steps, narrow, PITCH)
    rim_in = lambda r: [(r[0], spec_rows(narrow, 0, PITCH)), (r[1], spec_rows(narrow, 0, PITCH))]
    big = lambda: rows_out(steps, wide, space=HBM)
    mid = lambda: rows_out(steps, narrow)
    far = lambda: rows_out(steps, narrow, space=HBM)
    act0, slope0, act1, slope1, rims1 = [], [], [], [], []
    for c in chunks:
        a0, s0, a1, s1, *edges = image_call(
            partial(enter_kernel, offset=c * steps), "enter", scalars, steps,
            [(images, spec_slots(wide, c * steps)), (hat_in, spec_whole(hat_in)),
             (bias_in, spec_whole(bias_in))],
            [big(), big(), mid(), far(), rim(), rim()],
            [mask_scratch, flat_scratch], work,
        )
        act0.append(a0), slope0.append(s0), act1.append(a1), slope1.append(s1)
        rims1.append(neighbours(*edges))
    act2, slope2, rims2 = [], [], []
    for c in chunks:
        a2, s2, *edges = image_call(
            partial(conv_kernel, offset=c * steps), "conv_one", scalars, steps,
            [(act1[c], spec_rows(narrow)), *rim_in(rims1[c]), (fwd_one, spec_whole(fwd_one)),
             (bias_one, spec_whole(bias_one))],
            [mid(), far(), rim(), rim()],
            [tile_scratch, mask_scratch], conv_work,
        )
        act2.append(a2), slope2.append(s2)
        rims2.append(neighbours(*edges))
    act3, slope3, four, cotp, sums = [], [], [], [], []
    for c in chunks:
        a3, s3, z4, cp, partial_sums = image_call(
            partial(leave_kernel, offset=c * steps), "leave", scalars, steps,
            [(act2[c], spec_rows(narrow)), *rim_in(rims2[c]), (fwd_two, spec_whole(fwd_two)),
             (bias_two, spec_whole(bias_two)), (hat_out, spec_whole(hat_out)),
             (bias_out, spec_whole(bias_out)), (cotangent, spec_slots(wide, c * steps))],
            [mid(), far(), big(), big(),
             (jax.ShapeDtypeStruct((steps * 16, 2 * wide // 3), F32),
              pl.BlockSpec((16, 2 * wide // 3), lambda j, *_: (j, 0)))],
            [tile_scratch, mask_scratch, flat_scratch], work + conv_work,
        )
        act3.append(a3), slope3.append(s3), four.append(z4), cotp.append(cp)
        sums.append(rows_sum(partial_sums))
    seh = squeeze_weight.shape[1]
    inputs = [*sums, squeeze_weight, squeeze_bias, excite_weight, excite_bias]
    rows = CHUNKS * steps * 8
    scale, shift, factors = pl.pallas_call(
        gate_kernel,
        in_specs=[pl.BlockSpec(memory_space=pltpu.VMEM)] * len(inputs)
        + [pl.BlockSpec(memory_space=pltpu.SMEM)],
        out_shape=[
            jax.ShapeDtypeStruct((rows, wide), F32),
            jax.ShapeDtypeStruct((rows, wide), F32),
            jax.ShapeDtypeStruct((rows, 2 * wide + 2 * seh + 128), BF),
        ],
        compiler_params=PARAMS,
        cost_estimate=SMALL,
        name="gate",
    )(*inputs, skip_gain)

    def rims_all(c):
        shape = jax.ShapeDtypeStruct((count * PITCH, narrow), BF)
        return (shape, spec_rows(narrow, c * steps, PITCH))

    grad4, grad3, edges = [], [], []
    for c in chunks:
        d4, d3, *edges = image_call(
            partial(turn_kernel, offset=c * steps), "turn", scalars, steps,
            [(cotp[c], spec_rows(wide)), (scale, spec_sums(wide, c * steps)), (shift, spec_sums(wide, c * steps)),
             (hat_out, spec_whole(hat_out)), (slope3[c], spec_rows(narrow)),
             *[(edge, pl.BlockSpec(memory_space=pl.ANY)) for edge in edges]],
            [big(), mid(), rims_all(c), rims_all(c)],
            [mask_scratch], work, [(5, 2), (6, 3)] if edges else [],
        )
        grad4.append(d4), grad3.append(d3)
    rims3 = neighbours(*edges)

    factors = lax.all_gather(factors, "batch", axis=0, tiled=True)

    def run_output(c, held):
        alias = [] if held is None else [(held, pl.BlockSpec(memory_space=pl.ANY))]
        (out,) = image_call(
            partial(output_kernel, offset=c * steps), "output", scalars, steps,
            [(images, spec_slots(wide, c * steps)), (four[c], spec_rows(wide)),
             (scale, spec_sums(wide, c * steps)), *alias],
            [(HBM(images.shape, BF), spec_slots(wide, c * steps))], [flat_scratch], 0,
            [(3, 0)] if alias else [],
        )
        return out

    def run_grad_images(c, held):
        alias = [] if held is None else [(held, pl.BlockSpec(memory_space=pl.ANY))]
        (out,) = image_call(
            partial(grad_image_kernel, offset=c * steps), "grad_images", scalars, steps,
            [(grad1[c], spec_rows(narrow)), (hat_in, spec_whole(hat_in)),
             (slope0[c], spec_rows(wide)), (cotp[c], spec_rows(wide)), *alias],
            [(HBM(images.shape, BF), spec_slots(wide, c * steps))],
            [pltpu.VMEM((STEP * ROWS_IMG, wide), F32), flat_scratch], work, [(4, 0)] if alias else [],
        )
        return out

    groups = []

    def slot(run, value, *landing, rims=()):
        for group in groups:
            value = group.hold(value)
        value = run(value)
        for group in landing:
            value = group.land(value)
            if group.landed:
                groups.remove(group)
        for group in landing:
            if not group.landed:
                rims, group.send = ordered(rims, group.send)
                group.fly()
        return (value, rims) if rims else value

    def start(*blocks):
        group = Reduction(*blocks)
        group.fly()
        groups.append(group)
        return group

    def rims_of(rims, c):
        return [(rim, spec_rows(narrow, c * steps, PITCH)) for rim in rims]

    def run_back_two(c, edges, values):
        grad, rims = values
        return image_call(
            partial(conv_back_kernel, offset=c * steps, edged=True), "back_two", scalars, steps,
            [(grad, spec_rows(narrow)), *rims_of(rims, c), (fwd_two, spec_whole(fwd_two)),
             (slope2[c], spec_rows(narrow)), *[(edge, pl.BlockSpec(memory_space=pl.ANY)) for edge in edges]],
            [mid(), rims_all(c), rims_all(c)],
            [tile_scratch], conv_work, [(5, 1), (6, 2)] if edges else [],
        )

    def run_back_one(values):
        grads, rims = values
        return [
            image_call(
                partial(conv_back_kernel, offset=c * steps, edged=False), "back_one", scalars, steps,
                [(grads[c], spec_rows(narrow)), *rims_of(rims, c), (fwd_one, spec_whole(fwd_one)),
                 (slope1[c], spec_rows(narrow))],
                [mid()],
                [tile_scratch], conv_work,
            )[0]
            for c in chunks
        ]

    *part_out, vec_out = weight_flat(core, act3, grad4, proj_out, stat_out, narrow, "weight_out")
    rims3, part_out = ordered(rims3, part_out)
    group_out = start(part_out)
    first, *edges = slot(lambda values: run_back_two(0, [], values), (grad3[0], rims3), group_out)
    second, *edges = slot(lambda values: run_back_two(1, values[2], values[:2]), (grad3[1], rims3, edges))
    grad2, rims4 = [first, second], neighbours(*edges)
    conv_two_args = (act2, rims2, grad3, conv_two, stat_two)
    conv_one_args = (act1, rims1, grad2, conv_one, stat_one)
    two = slot(lambda args: weight_conv(core, scalars, *args, "weight_two"), conv_two_args)
    *part_two, vec_two = group_out.land(two)
    one = weight_conv(core, scalars, *group_out.hold(conv_one_args), "weight_one")
    rims4, (one, group_out.send) = ordered(rims4, (one, group_out.send))
    *part_one, vec_one = one
    group_out.fly()
    group_conv = start(part_one, part_two)
    grad1 = slot(run_back_one, (grad2, rims4), group_out, group_conv)
    *part_in, vec_in = slot(
        lambda grads: weight_flat(core, act0, grads, proj_in, stat_in, narrow, "weight_in"), grad1, group_out, group_conv
    )
    group_conv.send, part_in = ordered(group_conv.send, part_in)
    half = jax.ShapeDtypeStruct((4, 16, narrow), BF)
    part_vec = small_call(
        vector_kernel, "vectors", [core], [vec_in, vec_one, vec_two, vec_out], [half, half]
    )
    group_in = start(part_in, part_vec)

    def run_output(c, four_rows, held):
        alias = [] if held is None else [(held, pl.BlockSpec(memory_space=pl.ANY))]
        return image_call(
            partial(output_kernel, offset=c * steps), "output", scalars, steps,
            [(images, spec_slots(wide, c * steps)), (four_rows, spec_rows(wide)),
             (scale, spec_sums(wide, c * steps)), *alias],
            [(HBM(images.shape, BF), spec_slots(wide, c * steps))], [flat_scratch], 0,
            [(3, 0)] if alias else [],
        )[0]

    def run_grad_images(c, grads, held):
        alias = [] if held is None else [(held, pl.BlockSpec(memory_space=pl.ANY))]
        return image_call(
            partial(grad_image_kernel, offset=c * steps), "grad_images", scalars, steps,
            [(grads, spec_rows(narrow)), (hat_in, spec_whole(hat_in)),
             (slope0[c], spec_rows(wide)), (cotp[c], spec_rows(wide)), *alias],
            [(HBM(images.shape, BF), spec_slots(wide, c * steps))],
            [pltpu.VMEM((STEP * ROWS_IMG, wide), F32), flat_scratch], work, [(4, 0)] if alias else [],
        )[0]

    def spread(group, *shapes, vectors=()):
        def run(got):
            group.got = got
            return group.spread(*shapes, vectors=vectors)

        return run

    flat_conv = (9 * GW, narrow)
    grad_images = slot(lambda grads: run_grad_images(0, grads, None), grad1[0], group_in, group_out)
    grad_images = slot(lambda held: run_grad_images(1, grad1[1], held), grad_images, group_conv, group_out)
    output = slot(lambda rows: run_output(0, rows, None), four[0], group_in)
    output = slot(lambda held: run_output(1, four[1], held), output, group_conv, group_out)
    grad_ex_w, grad_ex_b = slot(lambda f: outer(f, wide + seh, seh, wide, "outer_excite"), factors, group_in)
    squeeze = slot(lambda f: outer(f, 0, wide, seh, "outer_squeeze", skip=True), factors, group_conv, group_out)
    assert group_out.landed
    (sum_out,) = slot(spread(group_out, proj_out.shape), group_out.got, group_in)
    for landing in (group_conv, group_in, group_conv, group_in, group_conv):
        sum_out = slot(lambda value: value, sum_out, landing)
    assert group_conv.landed
    sum_one, sum_two = slot(spread(group_conv, flat_conv, flat_conv), group_conv.got, group_in)
    while groups:
        sum_one = slot(lambda value: value, sum_one, group_in)
    grad_sq_w, grad_sq_b, skip_table = squeeze
    vectors = [(narrow,)] * 6 + [(wide,)] * 2
    sum_in, *vec = group_in.spread(proj_in.shape, vectors=vectors)
    return (
        output.transpose(0, 2, 1, 3),
        grad_images.transpose(0, 2, 1, 3),
        sum_in,
        vec[0],
        vec[1],
        sum_one.reshape(conv_one.shape),
        vec[2],
        vec[3],
        sum_two.reshape(conv_two.shape),
        vec[4],
        vec[5],
        sum_out,
        vec[6],
        vec[7],
        grad_sq_w,
        grad_sq_b,
        grad_ex_w,
        grad_ex_b,
        skip_table[0, :1],
    )


def solution(mesh):
    slots = P("batch", "rows", None, None)
    return jax.shard_map(
        shards,
        mesh=mesh,
        in_specs=(slots, P("batch"), slots) + (P(),) * 17,
        out_specs=(slots, slots) + (P(),) * 17,
        check_vma=False,
    )
```

```python
from functools import partial

import jax
import jax.numpy as jnp
from jax import lax
from jax.experimental import pallas as pl
from jax.experimental.pallas import tpu as pltpu
from jax.sharding import PartitionSpec as P

GW = 128
ROW_SLOTS = 4
COL_SLOTS = 14
PITCH = 16
ROWS_IMG = ROW_SLOTS * PITCH
TILE_IMG = ROWS_IMG + 2 * PITCH
PIXELS = 140
STEP = 5
CHUNKS = 2

GAMMA = 1.7015043497
BETA_SCALE = 0.9128709291752769
ALPHA = 0.2
WS_EPS = 1e-05
ROOT_HALF = 0.7071067811865476
INV_ROOT_TWO_PI = 0.3989422804014327
BF = jnp.bfloat16
F32 = jnp.float32
NN = (((1,), (0,)), ((), ()))
NT = (((1,), (1,)), ((), ()))
TN = (((0,), (0,)), ((), ()))
HBM = pltpu.HBM
SMALL = pl.CostEstimate(flops=1, bytes_accessed=1, transcendentals=0)
PARAMS = pltpu.CompilerParams(vmem_limit_bytes=28 * 2**20)


def dot(left, right, dims=NN):
    return lax.dot_general(left, right, dims, preferred_element_type=F32)


def normal_parts(signal):
    phi = 0.5 + 0.5 * lax.erf(signal * ROOT_HALF)
    bell = jnp.exp(-0.5 * signal * signal) * INV_ROOT_TWO_PI
    return phi, bell


def gelu_and_slope(signal):
    phi, bell = normal_parts(signal)
    return (GAMMA * signal) * phi, GAMMA * (phi + signal * bell)


def at_row(index):
    return pl.ds(pl.multiple_of(index * PITCH, PITCH), PITCH)


def lanes(mask, width):
    return jnp.concatenate([mask] * (width // 128), axis=1)


def slot_width(counts, widths, image, slot):
    return jnp.where(slot < counts[image], widths[image], 0)


def below(limit, shape):
    return lax.broadcasted_iota(jnp.int32, shape, 0) < limit


def fill_mask(counts, widths, base, mask_ref):
    for image in range(STEP):
        for slot in range(ROW_SLOTS):
            limit = slot_width(counts, widths, base + image, slot)
            row = image * ROW_SLOTS + slot
            mask_ref[row * PITCH : (row + 1) * PITCH, :] = below(limit, (PITCH, 128)).astype(F32)


def lane_tiles(width):
    return [(tile, slice(tile * 128, (tile + 1) * 128)) for tile in range(width // 128)]


def unpack_image(slots_ref, image, flat_ref):
    for col in range(COL_SLOTS):
        value = slots_ref[image, col].astype(F32)
        for tile, span in lane_tiles(value.shape[1]):
            flat_ref[tile, col * ROW_SLOTS : (col + 1) * ROW_SLOTS, :] = value[:, span]


def pack_image(flat_ref, slots_ref, image):
    for col in range(COL_SLOTS):
        rows = slice(col * ROW_SLOTS, (col + 1) * ROW_SLOTS)
        value = [flat_ref[tile, rows, :] for tile in range(flat_ref.shape[0])]
        slots_ref[image, col] = jnp.concatenate(value, axis=1).astype(BF)


def read_slot(flat_ref, slot):
    rows = pl.ds(slot, PITCH, stride=ROW_SLOTS)
    return jnp.concatenate([flat_ref[tile, rows, :] for tile in range(flat_ref.shape[0])], axis=1)


def write_slot(flat_ref, slot, value):
    rows = pl.ds(slot, PITCH, stride=ROW_SLOTS)
    for tile, span in lane_tiles(value.shape[1]):
        flat_ref[tile, rows, :] = value[:, span]


def clear_tail(flat_ref):
    first = ROW_SLOTS * COL_SLOTS
    flat_ref[:, first:, :] = jnp.zeros((flat_ref.shape[0], ROWS_IMG - first, 128), F32)


def store_edges(scalars, base, act_ref, even_ref, odd_ref):
    counts, _, place = scalars
    odd = place[0] == 1
    for image in range(STEP):
        dest = slice(image * PITCH, (image + 1) * PITCH)
        first = act_ref[image * ROWS_IMG : image * ROWS_IMG + PITCH, :]
        last = act_ref[at_row(image * ROW_SLOTS + counts[base + image] - 1), :]
        even_ref[dest, :] = jnp.where(odd, first, last)
        odd_ref[dest, :] = jnp.where(odd, last, first)


def fill_tile(scalars, base, act_ref, even_ref, odd_ref, tile_ref):
    counts, _, place = scalars
    odd = place[0] == 1
    tile_rows = TILE_IMG // PITCH
    for image in range(act_ref.shape[0] // ROWS_IMG):
        start = image * TILE_IMG
        rim = slice(image * PITCH, (image + 1) * PITCH)
        even, other = even_ref[rim, :], odd_ref[rim, :]
        tile_ref[start : start + PITCH, :] = jnp.where(odd, even, other)
        tile_ref[start + PITCH : start + PITCH + ROWS_IMG, :] = act_ref[
            image * ROWS_IMG : (image + 1) * ROWS_IMG, :
        ]
        tile_ref[start + PITCH + ROWS_IMG : start + TILE_IMG, :] = jnp.zeros(
            (PITCH, act_ref.shape[1]), act_ref.dtype
        )
        tile_ref[at_row(image * tile_rows + counts[base + image] + 1), :] = jnp.where(odd, other, even)


def group_cat(tile_ref, images, group):
    cols = slice(group * GW, (group + 1) * GW)
    return jnp.concatenate(
        [
            jnp.concatenate(
                [
                    tile_ref[
                        image * TILE_IMG + shift * PITCH : image * TILE_IMG + shift * PITCH + ROWS_IMG,
                        cols,
                    ]
                    for image in range(images)
                ],
                axis=0,
            )
            for shift in range(3)
        ],
        axis=1,
    )


def conv_group(tile_ref, images, group, weight, dims):
    wide = dot(group_cat(tile_ref, images, group), weight, dims)
    rows = wide.shape[0]
    return (
        wide[:, GW : 2 * GW]
        + pltpu.roll(wide[:, :GW], 1, 0)
        + pltpu.roll(wide[:, 2 * GW :], rows - 1, 0)
    )


def prep_flat_kernel(weight_ref, gain_ref, hat_ref, stat_ref):
    weight = weight_ref[...].astype(F32)
    fan = weight.shape[0]
    mean = jnp.sum(weight, axis=0, keepdims=True) * (1.0 / fan)
    center = weight - mean
    spread = jnp.sum(center * center, axis=0, keepdims=True) * (1.0 / fan)
    inv = lax.rsqrt(spread * fan + WS_EPS)
    gain = gain_ref[...][None, :]
    hat_ref[...] = (gain * center * inv).astype(BF)
    stat_ref[0:1, :] = mean
    stat_ref[1:2, :] = inv
    stat_ref[2:3, :] = gain


def prep_flat(weight, gain):
    fan, width = weight.shape
    block = 256
    return pl.pallas_call(
        prep_flat_kernel,
        grid=(width // block,),
        in_specs=[
            pl.BlockSpec((fan, block), lambda j: (0, j)),
            pl.BlockSpec((block,), lambda j: (j,)),
        ],
        out_specs=[
            pl.BlockSpec((fan, block), lambda j: (0, j)),
            pl.BlockSpec((8, block), lambda j: (0, j)),
        ],
        out_shape=[
            jax.ShapeDtypeStruct((fan, width), BF),
            jax.ShapeDtypeStruct((8, width), F32),
        ],
        compiler_params=PARAMS,
        name="prep_flat",
    )(weight, gain)


def prep_conv_kernel(weight_ref, gain_ref, fwd_ref, stat_ref):
    weight = weight_ref[...].astype(F32)
    fan = 9 * GW
    mean = jnp.sum(jnp.sum(weight, axis=0), axis=0, keepdims=True) * (1.0 / fan)
    center = weight - mean
    spread = jnp.sum(jnp.sum(center * center, axis=0), axis=0, keepdims=True) * (1.0 / fan)
    inv = lax.rsqrt(spread * fan + WS_EPS)
    gain = gain_ref[...][None, :]
    hat = (gain * center * inv).astype(BF)
    for row in range(3):
        for col in range(3):
            rows, cols = slice(row * GW, (row + 1) * GW), slice(col * GW, (col + 1) * GW)
            fwd_ref[0, rows, cols] = hat[3 * row + col]
    stat_ref[0:1, :] = mean
    stat_ref[1:2, :] = inv
    stat_ref[2:3, :] = gain


def prep_conv(weight, gain):
    width = weight.shape[2]
    groups = width // GW
    square = pl.BlockSpec((1, 3 * GW, 3 * GW), lambda j: (j, 0, 0))
    return pl.pallas_call(
        prep_conv_kernel,
        grid=(groups,),
        in_specs=[
            pl.BlockSpec((9, GW, GW), lambda j: (0, 0, j)),
            pl.BlockSpec((GW,), lambda j: (j,)),
        ],
        out_specs=[square, pl.BlockSpec((8, GW), lambda j: (0, j))],
        out_shape=[
            jax.ShapeDtypeStruct((groups, 3 * GW, 3 * GW), BF),
            jax.ShapeDtypeStruct((8, width), F32),
        ],
        compiler_params=PARAMS,
        name="prep_conv",
    )(weight, gain)


def spec_rows(width, offset=0, per=ROWS_IMG):
    return pl.BlockSpec((STEP * per, width), lambda j, *_: (j + offset, 0))


def spec_slots(width, offset):
    return pl.BlockSpec((STEP, COL_SLOTS, ROW_SLOTS, width), lambda j, *_: (j + offset, 0, 0, 0))


def spec_whole(array):
    zeros = (0,) * array.ndim
    return pl.BlockSpec(array.shape, lambda j, *_: zeros)


def spec_sums(width, offset):
    return pl.BlockSpec((8, width), lambda j, *_: (j + offset, 0))


def image_call(kernel, name, scalars, steps, inputs, outputs, scratch=(), flops=0, alias=()):
    return pl.pallas_call(
        kernel,
        grid_spec=pltpu.PrefetchScalarGridSpec(
            num_scalar_prefetch=len(scalars),
            grid=(steps,),
            in_specs=[spec for _, spec in inputs],
            out_specs=[spec for _, spec in outputs],
            scratch_shapes=list(scratch),
        ),
        out_shape=[shape for shape, _ in outputs],
        input_output_aliases={len(scalars) + source: target for source, target in alias},
        compiler_params=PARAMS,
        cost_estimate=SMALL,
        name=name,
    )(*scalars, *[array for array, _ in inputs])


def rows_out(steps, width, per=ROWS_IMG, dtype=BF, space=jax.ShapeDtypeStruct):
    return (space((steps * STEP * per, width), dtype), spec_rows(width, 0, per))


def enter_kernel(
    counts, widths, place, image_ref, hat_ref, bias_ref,
    act0_ref, slope0_ref, act1_ref, slope1_ref, even_ref, odd_ref, mask_ref, flat_ref, *, offset,
):
    base = (pl.program_id(0) + offset) * STEP
    fill_mask(counts, widths, base, mask_ref)
    clear_tail(flat_ref)

    def one_image(image, carry):
        unpack_image(image_ref, image, flat_ref)
        for slot in range(ROW_SLOTS):
            value = read_slot(flat_ref, slot)
            keep = below(slot_width(counts, widths, base + image, slot), value.shape)
            value = jnp.where(keep, value, 0.0)
            act, slope = gelu_and_slope(value)
            row = at_row(image * ROW_SLOTS + slot)
            act0_ref[row, :] = (act * BETA_SCALE).astype(BF)
            slope0_ref[row, :] = (slope * BETA_SCALE).astype(BF)
        return carry

    lax.fori_loop(0, STEP, one_image, 0)
    width = act1_ref.shape[1]
    block = 256
    keep = lanes(mask_ref[...], block)
    for start in range(0, width, block):
        cols = slice(start, start + block)
        pre = dot(act0_ref[...], hat_ref[:, cols]) + bias_ref[cols][None, :]
        act, slope = gelu_and_slope(pre)
        act1_ref[:, cols] = (act * keep).astype(BF)
        slope1_ref[:, cols] = (slope * keep).astype(BF)
    store_edges((counts, widths, place), base, act1_ref, even_ref, odd_ref)


def conv_body(tile_ref, weight_ref, bias_ref, out_ref, slope_ref, keep):
    for group in range(weight_ref.shape[0]):
        cols = slice(group * GW, (group + 1) * GW)
        pre = conv_group(tile_ref, STEP, group, weight_ref[group], NN) + bias_ref[cols][None, :]
        act, slope = gelu_and_slope(pre)
        out_ref[:, cols] = (act * keep).astype(BF)
        slope_ref[:, cols] = (slope * keep).astype(BF)


def conv_kernel(
    counts, widths, place, act_ref, up_ref, down_ref, weight_ref, bias_ref,
    out_ref, slope_ref, even_ref, odd_ref, tile_ref, mask_ref, *, offset,
):
    base = (pl.program_id(0) + offset) * STEP
    scalars = (counts, widths, place)
    fill_mask(counts, widths, base, mask_ref)
    fill_tile(scalars, base, act_ref, up_ref, down_ref, tile_ref)
    conv_body(tile_ref, weight_ref, bias_ref, out_ref, slope_ref, mask_ref[...])
    store_edges(scalars, base, out_ref, even_ref, odd_ref)


def leave_kernel(
    counts, widths, place, act_ref, up_ref, down_ref, weight_ref, bias_ref, hat_ref, bias_out_ref, cot_ref,
    out_ref, slope_ref, four_ref, cotp_ref, sum_ref, tile_ref, mask_ref, flat_ref, *, offset,
):
    base = (pl.program_id(0) + offset) * STEP
    fill_mask(counts, widths, base, mask_ref)
    fill_tile((counts, widths, place), base, act_ref, up_ref, down_ref, tile_ref)
    clear_tail(flat_ref)

    def one_image(image, carry):
        unpack_image(cot_ref, image, flat_ref)
        for slot in range(ROW_SLOTS):
            value = read_slot(flat_ref, slot)
            keep = below(slot_width(counts, widths, base + image, slot), value.shape)
            cotp_ref[at_row(image * ROW_SLOTS + slot), :] = jnp.where(keep, value, 0.0).astype(BF)
        return carry

    lax.fori_loop(0, STEP, one_image, 0)
    keep = mask_ref[...]
    conv_body(tile_ref, weight_ref, bias_ref, out_ref, slope_ref, keep)
    width = four_ref.shape[1]
    block = 256
    keep = lanes(keep, block)
    sum_ref[...] = jnp.zeros_like(sum_ref)
    third = sum_ref.shape[1]

    def put(values, image, column):
        row = column // third * STEP + image
        sum_ref[row : row + 1, column % third : column % third + block] = jnp.sum(
            values[image * ROWS_IMG : (image + 1) * ROWS_IMG], axis=0, keepdims=True
        )

    for start in range(0, width, block):
        cols = slice(start, start + block)
        pre = dot(out_ref[...], hat_ref[:, cols]) + bias_out_ref[cols][None, :]
        four_ref[:, cols] = pre.astype(BF)
        held = pre * keep
        cross = pre * cotp_ref[:, cols].astype(F32)
        for image in range(STEP):
            put(held, image, start)
            put(cross, image, width + start)


def unpacked_sums(*sum_refs):
    rows = []
    for sum_ref in sum_refs:
        for step in range(0, sum_ref.shape[0], 16):
            thirds = [sum_ref[step + STEP * t : step + STEP * (t + 1), :] for t in range(3)]
            rows.append(jnp.concatenate(thirds, axis=1))
            rows.append(jnp.zeros((8 - STEP, 3 * sum_ref.shape[1]), F32))
    return jnp.concatenate(rows, axis=0)


def two_pass(left, right, dims=NN):
    high = left.astype(BF)
    low = (left - high.astype(F32)).astype(BF)
    both = dot(jnp.concatenate([high, low], axis=0), right, dims)
    return both[: left.shape[0]] + both[left.shape[0] :]


def gate_kernel(
    sum0_ref, sum1_ref, squeeze_ref, squeeze_bias_ref, excite_ref, excite_bias_ref, skip_ref,
    scale_ref, shift_ref, factor_ref,
):
    width = scale_ref.shape[1]
    skip = skip_ref[0]
    sums = unpacked_sums(sum0_ref, sum1_ref)
    pooled = sums[:, :width] * (1.0 / PIXELS)
    cross = sums[:, width:] * ALPHA
    squeezed = two_pass(pooled, squeeze_ref[...]) + squeeze_bias_ref[...][None, :]
    phi, bell = normal_parts(squeezed)
    hidden = squeezed * phi
    excited = two_pass(hidden, excite_ref[...]) + excite_bias_ref[...][None, :]
    gate = 2.0 * jax.nn.sigmoid(excited)
    dexcite = (cross * skip) * gate * (1.0 - 0.5 * gate)
    dsqueeze = two_pass(dexcite, excite_ref[...], NT) * (phi + squeezed * bell)
    scale_ref[...] = (ALPHA * skip) * gate
    shift_ref[...] = two_pass(dsqueeze, squeeze_ref[...], NT) * (1.0 / PIXELS)
    dskip = jnp.sum(gate * cross, axis=1, keepdims=True)
    high = dskip.astype(BF).astype(F32)
    mid = (dskip - high).astype(BF).astype(F32)
    lane = lax.broadcasted_iota(jnp.int32, (dskip.shape[0], 128), 1)
    pieces = jnp.where(lane == 0, high, jnp.where(lane == 1, mid, dskip - high - mid))
    pieces = jnp.where(lane < 3, pieces, 0.0)
    factor_ref[...] = jnp.concatenate([pooled, dsqueeze, hidden, dexcite, pieces], axis=1).astype(BF)


def turn_kernel(
    counts, widths, place, cotp_ref, scale_ref, shift_ref, hat_ref, slope_ref, *rest, offset
):
    four_ref, three_ref, even_ref, odd_ref, mask_ref = rest[-5:]
    base = (pl.program_id(0) + offset) * STEP
    fill_mask(counts, widths, base, mask_ref)
    for image in range(STEP):
        rows = slice(image * ROWS_IMG, (image + 1) * ROWS_IMG)
        keep = lanes(mask_ref[rows, :], four_ref.shape[1])
        value = cotp_ref[rows, :].astype(F32) * scale_ref[image : image + 1, :]
        value = value + keep * shift_ref[image : image + 1, :]
        four_ref[rows, :] = value.astype(BF)
    width = three_ref.shape[1]
    block = 256
    for start in range(0, width, block):
        cols = slice(start, start + block)
        back = dot(four_ref[...], hat_ref[cols, :], NT)
        three_ref[:, cols] = (back * slope_ref[:, cols].astype(F32)).astype(BF)
    store_edges((counts, widths, place), base, three_ref, even_ref, odd_ref)


def turned(weight_ref, group):
    square = lambda row, col: weight_ref[
        group, (2 - row) * GW : (3 - row) * GW, (2 - col) * GW : (3 - col) * GW
    ]
    return jnp.concatenate(
        [jnp.concatenate([square(row, col) for row in range(3)], axis=1) for col in range(3)], axis=0
    )


def conv_back_kernel(
    counts, widths, place, grad_ref, up_ref, down_ref, weight_ref, slope_ref, *rest, offset, edged
):
    out_ref, *edges, tile_ref = rest[-4:] if edged else rest
    base = (pl.program_id(0) + offset) * STEP
    scalars = (counts, widths, place)
    fill_tile(scalars, base, grad_ref, up_ref, down_ref, tile_ref)
    for group in range(weight_ref.shape[0]):
        cols = slice(group * GW, (group + 1) * GW)
        back = conv_group(tile_ref, STEP, group, turned(weight_ref, group), NT)
        out_ref[:, cols] = (back * slope_ref[:, cols].astype(F32)).astype(BF)
    if edges:
        store_edges(scalars, base, out_ref, *edges)


def grad_image_kernel(counts, widths, place, grad_ref, hat_ref, slope_ref, cotp_ref, *rest, offset):
    out_ref, work_ref, flat_ref = rest[-3:]
    base = (pl.program_id(0) + offset) * STEP
    width = hat_ref.shape[0]
    block = 256
    for start in range(0, width, block):
        cols = slice(start, start + block)
        back = dot(grad_ref[...], hat_ref[cols, :], NT)
        work_ref[:, cols] = back * slope_ref[:, cols].astype(F32) + cotp_ref[:, cols].astype(F32)

    def one_image(image, carry):
        for slot in range(ROW_SLOTS):
            value = work_ref[at_row(image * ROW_SLOTS + slot), :]
            keep = below(slot_width(counts, widths, base + image, slot), value.shape)
            write_slot(flat_ref, slot, jnp.where(keep, value, 0.0))
        pack_image(flat_ref, out_ref, image)
        return carry

    lax.fori_loop(0, STEP, one_image, 0)


def output_kernel(counts, widths, place, image_ref, four_ref, scale_ref, *rest, offset):
    out_ref, flat_ref = rest[-2:]
    base = (pl.program_id(0) + offset) * STEP
    clear_tail(flat_ref)

    def one_image(image, carry):
        unpack_image(image_ref, image, flat_ref)
        for slot in range(ROW_SLOTS):
            value = read_slot(flat_ref, slot)
            four = four_ref[at_row(image * ROW_SLOTS + slot), :].astype(F32)
            keep = below(slot_width(counts, widths, base + image, slot), value.shape)
            value = jnp.where(keep, value + four * scale_ref[pl.ds(image, 1), :], 0.0)
            write_slot(flat_ref, slot, value)
        pack_image(flat_ref, out_ref, image)
        return carry

    lax.fori_loop(0, STEP, one_image, 0)


def split_halves(scratch_ref, core, keep_ref, send_ref):
    keep_ref[...] = scratch_ref[core]
    send_ref[...] = scratch_ref[1 - core]


def weight_flat_kernel(
    core, left0, left1, right0, right1, weight_ref, stat_ref, keep_ref, send_ref, vec_ref, scratch_ref
):
    pieces, rows, span = keep_ref.shape

    def store(start, grad):
        for first in range(0, grad.shape[0], rows):
            half, piece = divmod((start // span * grad.shape[0] + first) // rows, pieces)
            scratch_ref[half, piece, :, start % span : start % span + grad.shape[1]] = grad[
                first : first + rows
            ]

    weight_flat_body(left0, left1, right0, right1, weight_ref, stat_ref, store, vec_ref)
    split_halves(scratch_ref, core[0], keep_ref, send_ref)


def weight_flat_body(left0, left1, right0, right1, weight_ref, stat_ref, store, vec_ref):
    fan, width = weight_ref.shape
    block = 256
    vec_ref[...] = jnp.zeros_like(vec_ref)
    for start in range(0, width, block):
        cols = slice(start, start + block)
        ghat = dot(left0[...], right0[:, cols], TN) + dot(left1[...], right1[:, cols], TN)
        mean, inv, gain = stat_ref[0:1, cols], stat_ref[1:2, cols], stat_ref[2:3, cols]
        center = weight_ref[:, cols].astype(F32) - mean
        along = jnp.sum(ghat * center, axis=0, keepdims=True)
        level = jnp.sum(ghat, axis=0, keepdims=True) * (1.0 / fan)
        grad = ((gain * inv) * (ghat - level - center * (inv * inv * along))).astype(BF)
        store(start, grad)
        total = jnp.sum(right0[:, cols].astype(F32), axis=0, keepdims=True)
        total = total + jnp.sum(right1[:, cols].astype(F32), axis=0, keepdims=True)
        vec_ref[0:1, cols] = total
        vec_ref[1:2, cols] = inv * along


def halves_out(rows, span):
    shape = (4, rows // 8, span)
    return [jax.ShapeDtypeStruct(shape, BF)] * 2, pltpu.VMEM((2, *shape), BF)


def weight_call(kernel, name, scalars, inputs, rows, span, width, scratch, flops):
    halves, both = halves_out(rows, span)
    return pl.pallas_call(
        kernel,
        in_specs=[pl.BlockSpec(memory_space=pltpu.SMEM)] * len(scalars)
        + [pl.BlockSpec(memory_space=pltpu.VMEM)] * len(inputs),
        out_shape=[*halves, jax.ShapeDtypeStruct((8, width), F32)],
        scratch_shapes=[both, *scratch],
        compiler_params=PARAMS,
        cost_estimate=SMALL,
        name=name,
    )(*scalars, *inputs)


def weight_flat(core, lefts, rights, weight, stat, span, name):
    fan, width = weight.shape
    return weight_call(
        weight_flat_kernel, name, [core], [*lefts, *rights, weight, stat],
        fan * width // span, span, width, [], 4 * fan * width * lefts[0].shape[0],
    )


def weight_conv_kernel(
    core, counts, widths, place, act0, act1, even0, even1, odd0, odd1, grad0, grad1, weight_ref, stat_ref,
    keep_ref, send_ref, vec_ref, scratch_ref, tile_ref,
):
    images = act0.shape[0] // ROWS_IMG
    fan = 9 * GW
    scalars = (counts, widths, place)
    pieces, piece_rows, _ = keep_ref.shape
    fill_tile(scalars, 0, act0, even0, odd0, tile_ref.at[0])
    fill_tile(scalars, images, act1, even1, odd1, tile_ref.at[1])
    vec_ref[...] = jnp.zeros_like(vec_ref)
    for group in range(weight_ref.shape[2] // GW):
        cols = slice(group * GW, (group + 1) * GW)
        ghat = jnp.zeros((3 * GW, 3 * GW), F32)
        total = jnp.zeros((1, GW), F32)
        for index, grad_ref in enumerate((grad0, grad1)):
            grad = grad_ref[:, cols].astype(F32)
            rows = grad.shape[0]
            total = total + jnp.sum(grad, axis=0, keepdims=True)
            wide = jnp.concatenate(
                [
                    pltpu.roll(grad, rows - 1, 0).astype(BF),
                    grad_ref[:, cols],
                    pltpu.roll(grad, 1, 0).astype(BF),
                ],
                axis=1,
            )
            ghat = ghat + dot(group_cat(tile_ref.at[index], images, group), wide, TN)
        mean, inv, gain = stat_ref[0:1, cols], stat_ref[1:2, cols], stat_ref[2:3, cols]
        along = jnp.zeros((1, GW), F32)
        level = jnp.zeros((1, GW), F32)
        centers, taps = [], []
        for tap in range(9):
            row, col = tap // 3, tap % 3
            part = ghat[row * GW : (row + 1) * GW, col * GW : (col + 1) * GW]
            center = weight_ref[tap, :, cols].astype(F32) - mean
            along = along + jnp.sum(part * center, axis=0, keepdims=True)
            level = level + jnp.sum(part, axis=0, keepdims=True)
            centers.append(center)
            taps.append(part)
        level = level * (1.0 / fan)
        slope = inv * inv * along
        for tap in range(9):
            grad = ((gain * inv) * (taps[tap] - level - centers[tap] * slope)).astype(BF)
            row = 0
            while row < GW:
                whole, inside = divmod(tap * GW + row, piece_rows)
                half, piece = divmod(whole, pieces)
                size = min(piece_rows - inside, GW - row)
                scratch_ref[half, piece, inside : inside + size, cols] = grad[row : row + size]
                row += size
        vec_ref[0:1, cols] = total
        vec_ref[1:2, cols] = inv * along
    split_halves(scratch_ref, core[0], keep_ref, send_ref)


def weight_conv(core, scalars, acts, rims, grads, weight, stat, name):
    width = weight.shape[2]
    images = acts[0].shape[0] // ROWS_IMG
    inputs = [*acts, *[r[0] for r in rims], *[r[1] for r in rims], *grads, weight, stat]
    return weight_call(
        weight_conv_kernel, name, [core, *scalars], inputs, 9 * GW, width, width,
        [pltpu.VMEM((2, images * TILE_IMG, width), BF)], 36 * GW * width * acts[0].shape[0],
    )


def outer_kernel(factor_ref, out_ref, sum_ref, *skip, start):
    left, right = out_ref.shape
    factor = factor_ref[:, start + left : start + left + right]
    out_ref[...] = dot(factor_ref[:, start : start + left], factor, TN)
    sum_ref[...] = jnp.sum(factor.astype(F32), axis=0)
    for ref in skip:
        pieces = factor_ref[:, factor_ref.shape[1] - 128 :].astype(F32)
        ref[...] = jnp.broadcast_to(jnp.sum(pieces), ref.shape)


def outer(factors, start, left, right, name, skip=False):
    return pl.pallas_call(
        partial(outer_kernel, start=start),
        out_shape=[HBM((left, right), F32), jax.ShapeDtypeStruct((right,), F32)]
        + [jax.ShapeDtypeStruct((8, 128), F32)] * skip,
        compiler_params=PARAMS,
        cost_estimate=SMALL,
        name=name,
    )(factors)


def vector_kernel(core, in_ref, one_ref, two_ref, out_ref, keep_ref, send_ref):
    span = keep_ref.shape[2]
    keep_ref[...] = jnp.zeros_like(keep_ref)
    send_ref[...] = jnp.zeros_like(send_ref)
    rows = [ref[r : r + 1, :] for ref in (in_ref, one_ref, two_ref) for r in range(2)]
    rows += [out_ref[r : r + 1, c : c + span] for r in range(2) for c in range(0, out_ref.shape[1], span)]
    rows.append(jnp.zeros((16 - len(rows), span), F32))
    block = jnp.concatenate(rows, axis=0)
    keep_ref[0] = jnp.where(core[0] == 0, block, 0.0).astype(BF)
    send_ref[0] = jnp.where(core[0] == 0, 0.0, block).astype(BF)


def swap(block, axis, bit):
    count = lax.axis_size(axis)
    return lax.ppermute(block, axis, [(i, i ^ (1 << bit)) for i in range(count)])


def bit_of(axis, bit):
    return ((lax.axis_index(axis) >> bit) & 1).astype(jnp.int32)


def neighbours(even, odd):
    count = lax.axis_size("rows")
    inner = [(i, i + 1) for i in range(1, count - 1, 2)]
    outer_pairs = [(i, i + 1) for i in range(0, count, 2)]
    both = lambda pairs: pairs + [(target, source) for source, target in pairs]
    return lax.ppermute(even, "rows", both(outer_pairs)), lax.ppermute(odd, "rows", both(inner))


def rows_sum(total):
    for bit in range(lax.axis_size("rows").bit_length() - 1):
        total = total + swap(total, "rows", bit)
    return total


def orders():
    bits = lax.axis_size("batch").bit_length() - 1
    middle = 1 + (bits - 1) // 2
    along_x = [("batch", bit) for bit in range(1, middle)]
    along_y = [("batch", bit) for bit in range(middle, bits)]
    along_z = [("rows", bit) for bit in range(lax.axis_size("rows").bit_length() - 1)]
    return [along_x + along_y + along_z, along_y + along_z + along_x]


def swap_way(block, ways, step):
    rows = lax.axis_size("rows")
    pairs = []
    for index in range(lax.axis_size("batch") * rows):
        axis, bit = ways[(index // rows) & 1][step]
        pairs.append((index, index ^ ((rows if axis == "batch" else 1) << bit)))
    return lax.ppermute(block, ("batch", "rows"), pairs)


def small_call(kernel, name, scalars, inputs, outputs):
    return pl.pallas_call(
        kernel,
        in_specs=[pl.BlockSpec(memory_space=pltpu.SMEM)] * len(scalars)
        + [pl.BlockSpec(memory_space=pltpu.VMEM)] * len(inputs),
        out_shape=outputs,
        compiler_params=PARAMS,
        cost_estimate=SMALL,
        name=name,
    )(*scalars, *inputs)


def first_kernel(bits, *refs):
    sources, (kept, send) = refs[:-2], refs[-2:]
    mine = bits[0]
    for second in range(2):
        for index, dest in ((2 * mine + second, kept), (2 * (1 - mine) + second, send)):
            row = 0
            for keep, got in zip(sources[0::2], sources[1::2]):
                rows = keep.shape[1]
                value = keep[index].astype(F32) + got[index].astype(F32)
                dest[second, row : row + rows, :] = value.astype(dest.dtype)
                row += rows


def second_kernel(bits, kept, got, keep, send):
    mine = bits[1]
    keep[...] = kept[mine] + got[mine].astype(F32)
    send[...] = (kept[1 - mine] + got[1 - mine].astype(F32)).astype(BF)


def add_kernel(left, right, out):
    out[...] = (left[...].astype(F32) + right[...].astype(F32)).astype(BF)


def pair_kernel(left, right, out):
    out[0] = left[...]
    out[1] = right[...]


def join_kernel(left, right, out):
    out[0:2] = left[...]
    out[2:4] = right[...]


def spread_kernel(bits, own_ref, other_ref, *outs, vectors):
    pieces, _, span = own_ref.shape
    core = bits[2]
    if vectors:
        outs, lines, table = outs[: -1 - vectors], outs[-1 - vectors : -1], outs[-1]
        outs = [*outs, table]
    for piece in range(pieces):
        place = 2 * (bits[0] ^ (piece >> 1)) + (bits[1] ^ (piece & 1))
        other_place = 2 * (bits[3] ^ (piece >> 1)) + (bits[4] ^ (piece & 1))
        row = 0
        for out in outs:
            rows = out.shape[0] * out.shape[1] // (2 * pieces * span)
            if out.shape[1] == span:
                for half, where, ref in ((core, place, own_ref), (1 - core, other_place, other_ref)):
                    at = pl.ds(pl.multiple_of((half * pieces + where) * rows, rows), rows)
                    out[at, :] = ref[piece, row : row + rows].astype(F32)
            else:
                for half in range(2):

                    @pl.when(core == half)
                    def _(half=half, row=row, out=out, rows=rows):
                        for side, where, ref in ((half, place, own_ref), (1 - half, other_place, other_ref)):
                            at = pl.ds(pl.multiple_of(where * rows, rows), rows)
                            out[at, side * span : (side + 1) * span] = ref[piece, row : row + rows].astype(F32)

            row += rows
    if vectors:
        row = 0
        for out in lines:
            for start in range(0, out.shape[0], span):
                out[start : start + span] = table[row]
                row += 1


def interleave(left, right):
    return [item for pair in zip(left, right) for item in pair]


def ordered(before, after):
    flat_before, tree_before = jax.tree.flatten(before)
    flat_after, tree_after = jax.tree.flatten(after)
    out = lax.optimization_barrier((*flat_before, *flat_after))
    split = len(flat_before)
    return tree_before.unflatten(out[:split]), tree_after.unflatten(out[split:])


class Reduction:
    def __init__(self, *blocks):
        self.landed = False
        self.keep = [keep for keep, _ in blocks]
        self.send = [send for _, send in blocks]
        self.rows = [keep.shape[1] for keep in self.keep]
        rows, span = sum(self.rows), self.keep[0].shape[2]
        self.shape = lambda dtype, *lead: jax.ShapeDtypeStruct((*lead, rows, span), dtype)
        ways = orders()
        core = bit_of("batch", 0)
        mine = [[bit_of(*way[step]) for step in range(2)] for way in ways]
        choose = lambda step, which: jnp.where(core == which, mine[0][step], mine[1][step])
        self.bits = jnp.stack([choose(0, 0), choose(1, 0), core, choose(0, 1), choose(1, 1)])
        across = lambda step: lambda blocks: [swap_way(block, ways, step) for block in blocks]
        chip = lambda blocks: [swap(block, "batch", 0) for block in blocks]
        self.plan = [(chip, self.halve_first), (across(0), self.halve_second), (across(1), self.add_last)]
        self.plan += [(across(step), self.add_all) for step in (2, 3)]
        self.across, self.rest = across, range(4, len(ways[0]))
        self.plan += [(across(1), self.pair), (across(0), self.join), (chip, self.done)]

    def fly(self):
        self.move, self.work = self.plan.pop(0)
        self.got = self.move(self.send)

    def land(self, before):
        before, (self.keep, self.got) = ordered(before, (self.keep, self.got))
        self.work()
        return before

    def hold(self, after):
        self.send, after = ordered(self.send, after)
        return after

    def call(self, kernel, name, bits, left, right, outputs):
        return small_call(kernel, name, bits, interleave(left, right), outputs)

    def halve_first(self):
        outs = [self.shape(F32, 2), self.shape(BF, 2)]
        kept, send = self.call(first_kernel, "halve_first", [self.bits], self.keep, self.got, outs)
        self.keep, self.send = [kept], [send]

    def halve_second(self):
        outs = [self.shape(F32), self.shape(BF)]
        kept, send = self.call(second_kernel, "halve_second", [self.bits], self.keep, self.got, outs)
        self.keep, self.send = [kept], [send]

    def add_last(self):
        self.send = self.call(add_kernel, "add_last", [], self.keep, self.got, [self.shape(BF)])
        self.keep = []

    def add_all(self):
        self.send = self.call(add_kernel, "add_all", [], self.send, self.got, [self.shape(BF)])
        if self.plan[0][1] == self.pair:
            for step in self.rest:
                got = self.across(step)(self.send)
                self.send = self.call(add_kernel, "add_all", [], self.send, got, [self.shape(BF)])

    def pair(self):
        self.send = self.call(pair_kernel, "pair", [], self.send, self.got, [self.shape(BF, 2)])

    def join(self):
        self.send = self.call(join_kernel, "join", [], self.send, self.got, [self.shape(BF, 4)])

    def done(self):
        self.landed = True

    def spread(self, *shapes, vectors=()):
        inputs = [self.send[0], self.got[0]]
        return pl.pallas_call(
            partial(spread_kernel, vectors=len(vectors)),
            in_specs=[pl.BlockSpec(memory_space=pltpu.SMEM)] + [pl.BlockSpec(memory_space=pltpu.VMEM)] * 2,
            out_shape=[HBM(shape, F32) for shape in shapes]
            + [jax.ShapeDtypeStruct(shape, F32) for shape in vectors],
            scratch_shapes=[pltpu.VMEM((128, inputs[0].shape[2]), F32)] if vectors else [],
            compiler_params=PARAMS,
            cost_estimate=SMALL,
            name="spread",
        )(self.bits, *inputs)


def shards(
    images, orientation, cotangent, proj_in, bias_in, gain_in, conv_one, bias_one, gain_one,
    conv_two, bias_two, gain_two, proj_out, bias_out, gain_out, squeeze_weight, squeeze_bias,
    excite_weight, excite_bias, skip_gain,
):
    count = images.shape[0]
    wide, narrow = proj_in.shape
    steps = count // STEP // CHUNKS
    images = images.transpose(0, 2, 1, 3)
    cotangent = cotangent.transpose(0, 2, 1, 3)
    height = jnp.where(orientation == 0, 10, 14).astype(jnp.int32)
    widths = 24 - height
    row_index = lax.axis_index("rows")
    counts = height // 4 + (row_index < height % 4).astype(jnp.int32)
    core = bit_of("batch", 0).reshape(1)
    scalars = (counts, widths, (row_index % 2).astype(jnp.int32).reshape(1))
    mask_scratch = pltpu.VMEM((STEP * ROWS_IMG, 128), F32)
    tile_scratch = pltpu.VMEM((STEP * TILE_IMG, narrow), BF)
    flat_scratch = pltpu.VMEM((wide // 128, ROWS_IMG, 128), F32)
    work = 2 * steps * STEP * ROWS_IMG * wide * narrow
    conv_work = 2 * steps * STEP * ROWS_IMG * 12 * GW * narrow

    hat_in, stat_in = prep_flat(proj_in, gain_in)
    fwd_one, stat_one = prep_conv(conv_one, gain_one)
    fwd_two, stat_two = prep_conv(conv_two, gain_two)
    hat_out, stat_out = prep_flat(proj_out, gain_out)

    chunks = range(CHUNKS)
    rim = lambda: rows_out(steps, narrow, PITCH)
    rim_in = lambda r: [(r[0], spec_rows(narrow, 0, PITCH)), (r[1], spec_rows(narrow, 0, PITCH))]
    big = lambda: rows_out(steps, wide, space=HBM)
    mid = lambda: rows_out(steps, narrow)
    far = lambda: rows_out(steps, narrow, space=HBM)
    act0, slope0, act1, slope1, rims1 = [], [], [], [], []
    for c in chunks:
        a0, s0, a1, s1, *edges = image_call(
            partial(enter_kernel, offset=c * steps), "enter", scalars, steps,
            [(images, spec_slots(wide, c * steps)), (hat_in, spec_whole(hat_in)),
             (bias_in, spec_whole(bias_in))],
            [big(), big(), mid(), far(), rim(), rim()],
            [mask_scratch, flat_scratch], work,
        )
        act0.append(a0), slope0.append(s0), act1.append(a1), slope1.append(s1)
        rims1.append(neighbours(*edges))
    act2, slope2, rims2 = [], [], []
    for c in chunks:
        a2, s2, *edges = image_call(
            partial(conv_kernel, offset=c * steps), "conv_one", scalars, steps,
            [(act1[c], spec_rows(narrow)), *rim_in(rims1[c]), (fwd_one, spec_whole(fwd_one)),
             (bias_one, spec_whole(bias_one))],
            [mid(), far(), rim(), rim()],
            [tile_scratch, mask_scratch], conv_work,
        )
        act2.append(a2), slope2.append(s2)
        rims2.append(neighbours(*edges))
    act3, slope3, four, cotp, sums = [], [], [], [], []
    for c in chunks:
        a3, s3, z4, cp, partial_sums = image_call(
            partial(leave_kernel, offset=c * steps), "leave", scalars, steps,
            [(act2[c], spec_rows(narrow)), *rim_in(rims2[c]), (fwd_two, spec_whole(fwd_two)),
             (bias_two, spec_whole(bias_two)), (hat_out, spec_whole(hat_out)),
             (bias_out, spec_whole(bias_out)), (cotangent, spec_slots(wide, c * steps))],
            [mid(), far(), big(), big(),
             (jax.ShapeDtypeStruct((steps * 16, 2 * wide // 3), F32),
              pl.BlockSpec((16, 2 * wide // 3), lambda j, *_: (j, 0)))],
            [tile_scratch, mask_scratch, flat_scratch], work + conv_work,
        )
        act3.append(a3), slope3.append(s3), four.append(z4), cotp.append(cp)
        sums.append(rows_sum(partial_sums))
    seh = squeeze_weight.shape[1]
    inputs = [*sums, squeeze_weight, squeeze_bias, excite_weight, excite_bias]
    rows = CHUNKS * steps * 8
    scale, shift, factors = pl.pallas_call(
        gate_kernel,
        in_specs=[pl.BlockSpec(memory_space=pltpu.VMEM)] * len(inputs)
        + [pl.BlockSpec(memory_space=pltpu.SMEM)],
        out_shape=[
            jax.ShapeDtypeStruct((rows, wide), F32),
            jax.ShapeDtypeStruct((rows, wide), F32),
            jax.ShapeDtypeStruct((rows, 2 * wide + 2 * seh + 128), BF),
        ],
        compiler_params=PARAMS,
        cost_estimate=SMALL,
        name="gate",
    )(*inputs, skip_gain)

    def rims_all(c):
        shape = jax.ShapeDtypeStruct((count * PITCH, narrow), BF)
        return (shape, spec_rows(narrow, c * steps, PITCH))

    grad4, grad3, edges = [], [], []
    for c in chunks:
        d4, d3, *edges = image_call(
            partial(turn_kernel, offset=c * steps), "turn", scalars, steps,
            [(cotp[c], spec_rows(wide)), (scale, spec_sums(wide, c * steps)), (shift, spec_sums(wide, c * steps)),
             (hat_out, spec_whole(hat_out)), (slope3[c], spec_rows(narrow)),
             *[(edge, pl.BlockSpec(memory_space=pl.ANY)) for edge in edges]],
            [big(), mid(), rims_all(c), rims_all(c)],
            [mask_scratch], work, [(5, 2), (6, 3)] if edges else [],
        )
        grad4.append(d4), grad3.append(d3)
    rims3 = neighbours(*edges)

    factors = lax.all_gather(factors, "batch", axis=0, tiled=True)

    def run_output(c, held):
        alias = [] if held is None else [(held, pl.BlockSpec(memory_space=pl.ANY))]
        (out,) = image_call(
            partial(output_kernel, offset=c * steps), "output", scalars, steps,
            [(images, spec_slots(wide, c * steps)), (four[c], spec_rows(wide)),
             (scale, spec_sums(wide, c * steps)), *alias],
            [(HBM(images.shape, BF), spec_slots(wide, c * steps))], [flat_scratch], 0,
            [(3, 0)] if alias else [],
        )
        return out

    def run_grad_images(c, held):
        alias = [] if held is None else [(held, pl.BlockSpec(memory_space=pl.ANY))]
        (out,) = image_call(
            partial(grad_image_kernel, offset=c * steps), "grad_images", scalars, steps,
            [(grad1[c], spec_rows(narrow)), (hat_in, spec_whole(hat_in)),
             (slope0[c], spec_rows(wide)), (cotp[c], spec_rows(wide)), *alias],
            [(HBM(images.shape, BF), spec_slots(wide, c * steps))],
            [pltpu.VMEM((STEP * ROWS_IMG, wide), F32), flat_scratch], work, [(4, 0)] if alias else [],
        )
        return out

    groups = []

    def slot(run, value, *landing, rims=()):
        for group in groups:
            value = group.hold(value)
        value = run(value)
        for group in landing:
            value = group.land(value)
            if group.landed:
                groups.remove(group)
        for group in landing:
            if not group.landed:
                rims, group.send = ordered(rims, group.send)
                group.fly()
        return (value, rims) if rims else value

    def start(*blocks):
        group = Reduction(*blocks)
        group.fly()
        groups.append(group)
        return group

    def rims_of(rims, c):
        return [(rim, spec_rows(narrow, c * steps, PITCH)) for rim in rims]

    def run_back_two(c, edges, values):
        grad, rims = values
        return image_call(
            partial(conv_back_kernel, offset=c * steps, edged=True), "back_two", scalars, steps,
            [(grad, spec_rows(narrow)), *rims_of(rims, c), (fwd_two, spec_whole(fwd_two)),
             (slope2[c], spec_rows(narrow)), *[(edge, pl.BlockSpec(memory_space=pl.ANY)) for edge in edges]],
            [mid(), rims_all(c), rims_all(c)],
            [tile_scratch], conv_work, [(5, 1), (6, 2)] if edges else [],
        )

    def run_back_one(values):
        grads, rims = values
        return [
            image_call(
                partial(conv_back_kernel, offset=c * steps, edged=False), "back_one", scalars, steps,
                [(grads[c], spec_rows(narrow)), *rims_of(rims, c), (fwd_one, spec_whole(fwd_one)),
                 (slope1[c], spec_rows(narrow))],
                [mid()],
                [tile_scratch], conv_work,
            )[0]
            for c in chunks
        ]

    *part_out, vec_out = weight_flat(core, act3, grad4, proj_out, stat_out, narrow, "weight_out")
    rims3, part_out = ordered(rims3, part_out)
    group_out = start(part_out)
    first, *edges = slot(lambda values: run_back_two(0, [], values), (grad3[0], rims3), group_out)
    second, *edges = slot(lambda values: run_back_two(1, values[2], values[:2]), (grad3[1], rims3, edges))
    grad2, rims4 = [first, second], neighbours(*edges)
    conv_two_args = (act2, rims2, grad3, conv_two, stat_two)
    conv_one_args = (act1, rims1, grad2, conv_one, stat_one)
    two = slot(lambda args: weight_conv(core, scalars, *args, "weight_two"), conv_two_args)
    *part_two, vec_two = group_out.land(two)
    one = weight_conv(core, scalars, *group_out.hold(conv_one_args), "weight_one")
    rims4, (one, group_out.send) = ordered(rims4, (one, group_out.send))
    *part_one, vec_one = one
    group_out.fly()
    group_conv = start(part_one, part_two)
    grad1 = slot(run_back_one, (grad2, rims4), group_out, group_conv)
    def run_output(c, four_rows, held):
        alias = [] if held is None else [(held, pl.BlockSpec(memory_space=pl.ANY))]
        return image_call(
            partial(output_kernel, offset=c * steps), "output", scalars, steps,
            [(images, spec_slots(wide, c * steps)), (four_rows, spec_rows(wide)),
             (scale, spec_sums(wide, c * steps)), *alias],
            [(HBM(images.shape, BF), spec_slots(wide, c * steps))], [flat_scratch], 0,
            [(3, 0)] if alias else [],
        )[0]

    def run_in(grads):
        last = weight_flat(core, act0, grads, proj_in, stat_in, narrow, "weight_in")
        last, rows = ordered(last, four[0])
        return last, run_output(1, four[1], run_output(0, rows, None))

    (*part_in, vec_in), output = slot(run_in, grad1, group_out, group_conv)
    group_conv.send, part_in = ordered(group_conv.send, part_in)
    half = jax.ShapeDtypeStruct((4, 16, narrow), BF)
    part_vec = small_call(
        vector_kernel, "vectors", [core], [vec_in, vec_one, vec_two, vec_out], [half, half]
    )
    group_in = start(part_in, part_vec)

    def run_grad_images(c, grads, held):
        alias = [] if held is None else [(held, pl.BlockSpec(memory_space=pl.ANY))]
        return image_call(
            partial(grad_image_kernel, offset=c * steps), "grad_images", scalars, steps,
            [(grads, spec_rows(narrow)), (hat_in, spec_whole(hat_in)),
             (slope0[c], spec_rows(wide)), (cotp[c], spec_rows(wide)), *alias],
            [(HBM(images.shape, BF), spec_slots(wide, c * steps))],
            [pltpu.VMEM((STEP * ROWS_IMG, wide), F32), flat_scratch], work, [(4, 0)] if alias else [],
        )[0]

    def spread(group, *shapes, vectors=()):
        def run(got):
            group.got = got
            return group.spread(*shapes, vectors=vectors)

        return run

    flat_conv = (9 * GW, narrow)
    grad_images = slot(lambda grads: run_grad_images(0, grads, None), grad1[0], group_in, group_out)
    grad_images = slot(lambda held: run_grad_images(1, grad1[1], held), grad_images, group_conv, group_out)
    grad_ex_w, grad_ex_b = slot(lambda f: outer(f, wide + seh, seh, wide, "outer_excite"), factors, group_in)
    squeeze = slot(lambda f: outer(f, 0, wide, seh, "outer_squeeze", skip=True), factors, group_conv, group_out)
    squeeze = slot(lambda value: value, squeeze, group_in)
    squeeze = slot(lambda value: value, squeeze, group_conv, group_out)
    assert group_out.landed
    (sum_out,) = slot(spread(group_out, proj_out.shape), group_out.got, group_in)
    for landing in (group_conv, group_in, group_conv, group_in, group_conv):
        sum_out = slot(lambda value: value, sum_out, landing)
    assert group_conv.landed
    sum_one, sum_two = slot(spread(group_conv, flat_conv, flat_conv), group_conv.got, group_in)
    while groups:
        sum_one = slot(lambda value: value, sum_one, group_in)
    grad_sq_w, grad_sq_b, skip_table = squeeze
    vectors = [(narrow,)] * 6 + [(wide,)] * 2
    sum_in, *vec = group_in.spread(proj_in.shape, vectors=vectors)
    return (
        output.transpose(0, 2, 1, 3),
        grad_images.transpose(0, 2, 1, 3),
        sum_in,
        vec[0],
        vec[1],
        sum_one.reshape(conv_one.shape),
        vec[2],
        vec[3],
        sum_two.reshape(conv_two.shape),
        vec[4],
        vec[5],
        sum_out,
        vec[6],
        vec[7],
        grad_sq_w,
        grad_sq_b,
        grad_ex_w,
        grad_ex_b,
        skip_table[0, :1],
    )


def solution(mesh):
    slots = P("batch", "rows", None, None)
    return jax.shard_map(
        shards,
        mesh=mesh,
        in_specs=(slots, P("batch"), slots) + (P(),) * 17,
        out_specs=(slots, slots) + (P(),) * 17,
        check_vma=False,
    )
```
